256 devices in a mesh: gx: 8 (over y_lo, x), gy: 16 (over z, core), gz: 2 (over y_hi).
Axes of the slice: x: 4, y: 4 (y_hi: 2, y_lo: 2; y = y_hi * 2 + y_lo), z: 8, core: 2. Of those that a mesh axis runs over, the one named last changes fastest.
Arguments:
- velocity: float32 [3, 64, 512, 256], P(None, 'gx', 'gy', 'gz'), may hold values from -6 to 6
- fibre_vel: float32 [3, 8388608], P(None, ('gx', 'gy', 'gz')), may hold values from -6 to 6
- fluid_vel: float32 [3, 8388608], P(None, ('gx', 'gy', 'gz')), may hold values from -6 to 6
- fibre_props: float32 [2, 8388608], P(None, ('gx', 'gy', 'gz')), may hold values from 0.2 to 2
- fibre_row: int32 [8388608], P(('gx', 'gy', 'gz')), may hold values from 0 to 255
- fibre_height: int32 [8388608], P(('gx', 'gy', 'gz')), may hold values from 0 to 127
- migrant_list: int32 [4, 262144], P(None, ('gx', 'gy', 'gz')), may hold values from 0 to 32767, as said below
- migrant_slot: int32 [4, 262144], P(None, ('gx', 'gy', 'gz')), may hold values from 0 to 15
- side_rows: int32 [4, 4096], P(None, ('gx', 'gy', 'gz')), may hold values from 0 to 255, as said below
Outputs:
- new_velocity: float32 [3, 64, 512, 256], P(None, 'gx', 'gy', 'gz')
- kept_fibres: float32 [3, 8388608], P(None, ('gx', 'gy', 'gz'))
- arrivals: float32 [4, 3, 262144], P(None, None, ('gx', 'gy', 'gz'))
The draws below stay inside these ranges and needn't reach their ends.
Inputs may be any that keep to these rules, and one draw needn't show every extreme that they name: `migrant_list`: the 4096 entries that one brick holds are distinct numbers of fibres of that brick. `side_rows`: row numbers x * 32 + y of the neighbour brick in the list's direction; distinct within one list of one brick. `fibre_row`: A row of the fibre's own brick; not used for a fibre that moves. `migrant_slot`: A slot of the row list of the same direction and brick.
All inputs are finite; a program needn't handle non-finite values.
Results may differ from the reference program's by a relative error of at most 0.00002.
Values sent between devices are 32-bit elements; how exact they have to be, the bound alone decides.
No kernel may reach another device: no remote copies, remote signals or barrier semaphores. Data moves between devices by JAX's collectives and lax.ppermute only.
A program may use at most 256 MiB of HBM per device.

```python
import math
import jax
import jax.numpy as jnp
from jax import lax

CX = 8
CY = 32
CZ = 128
FIB_DEV = 32768
MIG = 1024
CAP = 16
SWEEPS = 3
NX = 64
NY = 512
NZ = 256
FIBRES = 8388608
MIGS = 262144
SLOTS = 4096
N_GX = 8
N_GY = 16
N_GZ = 2


def pick_distinct(key, groups, pool, count):
    keys = jax.random.split(key, groups)
    picked = jax.vmap(lambda one_key: jax.random.permutation(one_key, pool)[:count])(keys)
    return picked.astype(jnp.int32)


def draw_migrant_list(key, part):
    device_total = MIGS // MIG
    picked = pick_distinct(jax.random.fold_in(key, 11), device_total, FIB_DEV, 4 * MIG)
    return picked.reshape(device_total, 4, MIG).transpose(1, 0, 2).reshape(4, MIGS)


def draw_side_rows(key, part):
    device_total = SLOTS // CAP
    picked = pick_distinct(jax.random.fold_in(key, 23), device_total * 4, CX * CY, CAP)
    return picked.reshape(device_total, 4, CAP).transpose(1, 0, 2).reshape(4, SLOTS)


def set_ends(values, rng, smallest, top_value):
    index_at = [jax.random.randint(jax.random.fold_in(rng, axis), (), 0, length) for axis, length in enumerate(values.shape)]
    widest = values.shape.index(max(values.shape))
    beside = index_at[:widest] + [(index_at[widest] + 1) % values.shape[widest]] + index_at[widest + 1:]
    return values.at[tuple(index_at)].set(smallest).at[tuple(beside)].set(top_value)


def levels(rng, extent, pieces, least, top_value):
    def one(dim, parts):
        draws = jax.random.uniform(jax.random.fold_in(jax.random.fold_in(rng, 6), dim), (parts,), jnp.float32, least / len(pieces), top_value / len(pieces))
        return jnp.repeat(jnp.exp(draws), extent[dim] // parts).reshape((-1,) + (1,) * (len(extent) - dim - 1))

    loudness = one(*pieces[0])
    for cut in pieces[1:]:
        loudness = loudness * one(*cut)
    return loudness


def normal_values(key, extent, width, most, pieces=(), kind=jnp.bfloat16):
    gain = levels(key, extent, pieces, -0.22, 0.18) if pieces else 1.0
    entries = jax.random.normal(key, extent, jnp.float32) * width * gain
    return jnp.minimum(jnp.maximum(entries, -most), most).astype(kind)


def setup_inputs(seed: int = 0) -> dict:
    key_list = jax.random.split(jax.random.key(seed), 10)
    velocity = normal_values(key_list[0], (3, NX, NY, NZ), 1.0, 6.0, ((1, 8), (2, 16), (3, 2)), jnp.float32)
    fibre_vel = normal_values(key_list[1], (3, FIBRES), 1.0, 6.0, ((1, 256),), jnp.float32)
    fluid_vel = normal_values(key_list[2], (3, FIBRES), 1.0, 6.0, ((1, 256),), jnp.float32)
    fibre_props = jnp.clip(jnp.exp(math.log(2.0) - 2.3025851 * jax.random.uniform(key_list[3], (2, FIBRES), jnp.float32) ** levels(key_list[3], (2, FIBRES), ((1, 256),), -0.2, 0.2)), 0.2, 2.0)
    fibre_row = set_ends(jax.random.randint(key_list[4], (FIBRES,), 0, CX * CY), jax.random.fold_in(key_list[4], 1), 0, (CX * CY) - 1).astype(jnp.int32)
    fibre_height = set_ends(jax.random.randint(key_list[5], (FIBRES,), 0, CZ), jax.random.fold_in(key_list[5], 1), 0, CZ - 1).astype(jnp.int32)
    migrant_list = draw_migrant_list(jax.random.fold_in(key_list[9], 71), 0)
    migrant_slot = set_ends(jax.random.randint(key_list[7], (4, MIGS), 0, CAP), jax.random.fold_in(key_list[7], 1), 0, CAP - 1).astype(jnp.int32)
    side_rows = draw_side_rows(jax.random.fold_in(key_list[9], 71), 0)
    return dict(velocity=velocity, fibre_vel=fibre_vel, fluid_vel=fluid_vel, fibre_props=fibre_props, fibre_row=fibre_row, fibre_height=fibre_height, migrant_list=migrant_list, migrant_slot=migrant_slot, side_rows=side_rows)


drag_step = 0.25
source_step = 1.0
coupling = 1.0


def fibre_terms(fibre_vel, fluid_vel, fibre_props):
    volume = fibre_props[0][None, :]
    drag_force = fibre_props[1][None, :] * (fluid_vel - fibre_vel)
    moved_vel = fibre_vel + drag_step * drag_force / volume
    partials = jnp.concatenate([drag_force, volume], axis=0)
    return partials, moved_vel


def adjacent_value(grid_field, axis_location, upper_value):
    leading = grid_field.ndim - 3
    result = grid_field
    for position in range(3):
        length = grid_field.shape[leading + position]
        start = 1
        if position == axis_location:
            start = 2 if upper_value else 0
        result = lax.slice_in_dim(result, start, start + length - 2, axis=leading + position)
    return result


def relaxation_pass(bordered_velocity, bordered_porosity, momentum_source):
    central_value = bordered_porosity[1:-1, 1:-1, 1:-1]
    weight_sum = jnp.zeros_like(central_value)
    flux_sum = jnp.zeros_like(momentum_source)
    for axis_location in range(3):
        for upper_value in (False, True):
            blend_weight = 0.5 * (central_value + adjacent_value(bordered_porosity, axis_location, upper_value))
            weight_sum = weight_sum + blend_weight
            flux_sum = flux_sum + blend_weight[None] * adjacent_value(bordered_velocity, axis_location, upper_value)
    return (momentum_source + coupling * flux_sum) / (central_value + coupling * weight_sum)[None]


def by_device(values, dev_total):
    leading = values.shape[0]
    return values.reshape(leading, dev_total, -1).transpose(1, 0, 2)


def reference(velocity, fibre_vel, fluid_vel, fibre_props, fibre_row, fibre_height, migrant_list, migrant_slot, side_rows):
    grid_shape = (N_GX, N_GY, N_GZ)
    dev_total = N_GX * N_GY * N_GZ
    row_count = CX * CY
    cell_count = row_count * CZ
    vel_dev = by_device(fibre_vel, dev_total)
    fluid_dev = by_device(fluid_vel, dev_total)
    props_dev = by_device(fibre_props, dev_total)
    cell_dev = (fibre_row * CZ + fibre_height).astype(jnp.int32).reshape(dev_total, FIB_DEV)
    height_dev = fibre_height.reshape(dev_total, FIB_DEV)
    list_dev = by_device(migrant_list, dev_total)
    slot_dev = by_device(migrant_slot, dev_total)
    rows_dev = by_device(side_rows, dev_total)

    def local_part(vel_one, fluid_one, props_one, cell_one, height_one, list_one, slot_one):
        partials, moved_vel = fibre_terms(vel_one, fluid_one, props_one)
        staying = jnp.ones((FIB_DEV,), jnp.float32).at[list_one.reshape(-1)].set(0.0)
        kept_vel = moved_vel * staying[None, :]
        deposit = jnp.zeros((4, cell_count), jnp.float32).at[:, cell_one].add(partials * staying[None, :])
        slot_cells = slot_one * CZ + height_one[list_one]
        moving = partials[:, list_one].transpose(1, 0, 2)

        def one_block(cell_ids, part_terms):
            return jnp.zeros((4, CAP * CZ), jnp.float32).at[:, cell_ids].add(part_terms).reshape(4, CAP, CZ)

        blocks = jax.vmap(one_block)(slot_cells, moving)
        movers = moved_vel[:, list_one].transpose(1, 0, 2)
        return kept_vel, deposit, blocks, movers

    kept_vel, deposit, blocks, movers = jax.vmap(local_part)(vel_dev, fluid_dev, props_dev, cell_dev, height_dev, list_dev, slot_dev)

    def add_rows(total_one, rows_one, ids_one):
        return total_one.reshape(4, row_count, CZ).at[:, ids_one].add(rows_one).reshape(4, cell_count)

    arrived = []
    for direction in range(4):
        grid_axis = direction // 2
        step_by = 1 if direction % 2 == 1 else -1

        def neighbour(values):
            spread = values.reshape(grid_shape + values.shape[1:])
            return jnp.roll(spread, step_by, axis=grid_axis).reshape(values.shape)

        got_rows = neighbour(blocks[:, direction])
        got_ids = neighbour(rows_dev[:, direction])
        arrived.append(neighbour(movers[:, direction]))
        deposit = jax.vmap(add_rows)(deposit, got_rows, got_ids)

    field = deposit.reshape(grid_shape + (4, CX, CY, CZ)).transpose(3, 0, 4, 1, 5, 2, 6).reshape(4, NX, NY, NZ)
    void_fraction = 1.0 / (1.0 + field[3])
    momentum_source = void_fraction[None] * velocity - source_step * field[0:3]
    bordered_porosity = jnp.pad(jnp.pad(void_fraction, ((1, 1), (1, 1), (0, 0)), mode="wrap"), ((0, 0), (0, 0), (1, 1)), constant_values=1.0)
    present_velocity = velocity
    for sweep_index in range(SWEEPS):
        bordered_velocity = jnp.pad(jnp.pad(present_velocity, ((0, 0), (1, 1), (1, 1), (0, 0)), mode="wrap"), ((0, 0), (0, 0), (0, 0), (1, 1)))
        present_velocity = relaxation_pass(bordered_velocity, bordered_porosity, momentum_source)
    kept_fibres = kept_vel.transpose(1, 0, 2).reshape(3, FIBRES)
    arrivals = jnp.stack(arrived, axis=0).transpose(0, 2, 1, 3).reshape(4, 3, MIGS)
    return present_velocity, kept_fibres, arrivals
```

```python
import jax
import jax.numpy as jnp
from jax import lax
from jax.experimental import pallas as pl
from jax.experimental.pallas import tpu as pltpu
from jax.sharding import PartitionSpec as P

F32 = jnp.float32
BF16 = jnp.bfloat16
NT = (((1,), (1,)), ((), ()))
drag_step = 0.25
source_step = 1.0
coupling = 1.0
SWEEPS = 3
MIB = 2**20


def two_parts(value):
    high = value.astype(BF16)
    return high, (value - high.astype(F32)).astype(BF16)


def one_hot(index_row, count):
    ids = lax.broadcasted_iota(jnp.int32, (count, index_row.shape[1]), 0)
    return jnp.where(ids == index_row, 1.0, 0.0).astype(BF16)


def fibre_kernel(
    vel_ref, fluid_ref, props_ref, row_ref, height_ref, list_ref, slot_ref, ids_ref, grid_ref, back_ref,
    kept_ref, table_ref, place_ref, x_low, x_high, y_low, y_high, z_face, hot_ref, stay_ref,
):
    tiles = row_ref.shape[0]
    movers = list_ref.shape[1]
    packs = (x_low, x_high, y_low, y_high)
    slots = ids_ref.shape[1]
    hits = jnp.zeros((tiles, 128), F32)
    for d in range(4):
        named = list_ref[d : d + 1, :]
        tile_hot = one_hot(named // 128, tiles)
        hot_ref[d, 0:tiles, :] = tile_hot
        hot_ref[d, tiles : 2 * tiles, :] = tile_hot
        hits += lax.dot_general(
            tile_hot, one_hot(named % 128, 128), NT, preferred_element_type=F32
        )
    stay_ref[...] = 1.0 - hits
    place_ref[...] = jnp.where(hits > 0.5, -1.0, row_ref[...].astype(F32))

    def terms(block, _):
        for inner in range(8):
            tile = block * 8 + inner
            lanes = pl.ds(pl.multiple_of(tile * 128, 128), 128)
            vel = vel_ref[:, lanes]
            volume = props_ref[0:1, lanes]
            force = props_ref[1:2, lanes] * (fluid_ref[:, lanes] - vel)
            moved = vel + drag_step * force / volume
            kept_ref[:, lanes] = moved * stay_ref[pl.ds(tile, 1), :]
            table_ref[pl.ds(tile * 8, 3), :] = force
            table_ref[pl.ds(tile * 8 + 3, 1), :] = volume
            table_ref[pl.ds(tile * 8 + 4, 3), :] = moved
            table_ref[pl.ds(tile * 8 + 7, 1), :] = height_ref[pl.ds(tile, 1), :].astype(F32)
        return 0

    lax.fori_loop(0, tiles // 8, terms, 0)
    tables = []
    for f in range(8):
        field = table_ref[pl.ds(f, tiles, stride=8), :].T
        high, low = two_parts(field)
        tables.append(jnp.concatenate([high, low], axis=1))
    lane_ids = lax.broadcasted_iota(jnp.int32, (128, movers), 0)
    for d in range(4):
        lane_hit = lane_ids == list_ref[d : d + 1, :] % 128
        picked = []
        for f in range(8):
            columns = jnp.dot(tables[f], hot_ref[d], preferred_element_type=F32)
            picked.append(jnp.sum(jnp.where(lane_hit, columns, 0.0), axis=0, keepdims=True))
        at_height = lane_ids == picked[7].astype(jnp.int32)
        slot_hot = one_hot(slot_ref[d : d + 1, :], slots)
        for f in range(4):
            high, low = two_parts(picked[f])
            spread = jnp.concatenate(
                [
                    jnp.where(at_height, high.astype(F32), 0.0).astype(BF16),
                    jnp.where(at_height, low.astype(F32), 0.0).astype(BF16),
                ],
                axis=0,
            )
            rows = lax.dot_general(slot_hot, spread, NT, preferred_element_type=F32)
            packs[d][f * slots : (f + 1) * slots, :] = rows[:, 0:128] + rows[:, 128:256]
        at = 4 * slots
        packs[d][at : at + 8, :] = jnp.zeros((8, 128), F32)
        packs[d][at : at + 1, 0:slots] = ids_ref[d : d + 1, :].astype(F32)
        at += 8
        for f in range(3):
            for t in range(movers // 128):
                packs[d][at : at + 1, :] = picked[4 + f][:, t * 128 : (t + 1) * 128]
                at += 1
    x_width, y_width = grid_ref.shape[1], grid_ref.shape[2]
    base = 4 * slots + 8 + 3 * (movers // 128)
    for f in range(3):
        x_low[base + f * y_width : base + (f + 1) * y_width, :] = grid_ref[f, 0]
        x_high[base + f * y_width : base + (f + 1) * y_width, :] = grid_ref[f, x_width - 1]
        for x in range(x_width):
            at = base + f * x_width + x
            y_low[at : at + 1, :] = grid_ref[f, x, 0:1, :]
            y_high[at : at + 1, :] = grid_ref[f, x, y_width - 1 : y_width, :]
    write_z_face(z_face, [grid_ref[f].reshape(x_width * y_width, 128) for f in range(3)], back_ref)


def write_z_face(face_ref, fields, back_ref):
    face_ref[...] = jnp.zeros(face_ref.shape, F32)
    back = back_ref[0] > 0
    for f, field in enumerate(fields):
        turned = field.T
        face_ref[f : f + 1, :] = jnp.where(back, turned[0:1, :], turned[127:128, :])


def fibre_part(vel, fluid, props, row, height, lists, slots, ids, velocity, back):
    tiles = row.shape[0]
    movers = lists.shape[1]
    cap = ids.shape[1]
    x_width, y_width = velocity.shape[1], velocity.shape[2]
    base = 4 * cap + 8 + 3 * (movers // 128)
    x_rows, y_rows = base + 3 * y_width, base + 3 * x_width
    vmem = pl.BlockSpec(memory_space=pltpu.VMEM)
    shape = jax.ShapeDtypeStruct
    return pl.pallas_call(
        fibre_kernel,
        in_specs=[vmem] * 9 + [pl.BlockSpec(memory_space=pltpu.SMEM)],
        out_shape=[
            shape(vel.shape, F32),
            shape((tiles * 8, 128), F32),
            shape((tiles, 128), F32),
            shape((x_rows, 128), F32),
            shape((x_rows, 128), F32),
            shape((y_rows, 128), F32),
            shape((y_rows, 128), F32),
            shape((8, x_width * y_width), F32),
        ],
        out_specs=[vmem] * 8,
        scratch_shapes=[pltpu.VMEM((4, 2 * tiles, movers), BF16), pltpu.VMEM((tiles, 128), F32)],
        compiler_params=pltpu.CompilerParams(vmem_limit_bytes=48 * MIB),
        cost_estimate=pl.CostEstimate(flops=10**9, bytes_accessed=4 * MIB, transcendentals=0),
        name="fibre_terms",
    )(vel, fluid, props, row, height, lists, slots, ids, velocity, back)


def spread_tiles(table_ref, place_ref, values_ref, rows_ref, tiles):
    ids = lax.broadcasted_iota(jnp.int32, (16, 128), 0).astype(F32).astype(BF16)
    zero = jnp.zeros((16, 128), BF16)
    one = jnp.ones((16, 128), BF16)
    row_groups = rows_ref.shape[0] // 16
    for c in range(tiles):
        lanes = slice(c * 128, (c + 1) * 128)
        place = jnp.broadcast_to(place_ref[c : c + 1, :], (16, 128)).astype(BF16)
        for i in range(row_groups):
            rows_ref[16 * i : 16 * i + 16, lanes] = jnp.where(ids + BF16(16 * i) == place, one, zero)
        height = jnp.broadcast_to(table_ref[8 * c + 7 : 8 * c + 8, :], (16, 128)).astype(BF16)
        parts = []
        for f in range(4):
            parts.extend(two_parts(jnp.broadcast_to(table_ref[8 * c + f : 8 * c + f + 1, :], (16, 128))))
        for i in range(8):
            hit = ids + BF16(16 * i) == height
            for p in range(8):
                at = 128 * p + 16 * i
                values_ref[at : at + 16, lanes] = jnp.where(hit, parts[p], zero)


def deposit_kernel(table_ref, place_ref, out_ref, values_a, rows_a, values_b, rows_b, total, *, tiles):
    steps = place_ref.shape[0] // tiles
    total[...] = jnp.zeros_like(total)

    def fill(step, values, rows):
        spread_tiles(
            table_ref.at[pl.ds(pl.multiple_of(step * 8 * tiles, 8 * tiles), 8 * tiles), :],
            place_ref.at[pl.ds(pl.multiple_of(step * tiles, 8), tiles), :],
            values, rows, tiles,
        )

    fill(0, values_a, rows_a)

    def pair(j, _):
        part = lax.dot_general(values_a[...], rows_a[...], NT, preferred_element_type=F32)
        fill(2 * j + 1, values_b, rows_b)
        total[...] += part
        part = lax.dot_general(values_b[...], rows_b[...], NT, preferred_element_type=F32)
        fill(lax.rem(2 * j + 2, steps), values_a, rows_a)
        total[...] += part
        return 0

    lax.fori_loop(0, steps // 2, pair, 0)
    for f in range(4):
        at = 256 * f
        out_ref[f] = (total[at : at + 128, :] + total[at + 128 : at + 256, :]).T


def deposit_part(table, place, cells_x_y):
    tiles = 8
    return pl.pallas_call(
        lambda *refs: deposit_kernel(*refs, tiles=tiles),
        out_shape=jax.ShapeDtypeStruct((4, cells_x_y, 128), F32),
        scratch_shapes=[
            pltpu.VMEM((1024, 128 * tiles), BF16),
            pltpu.VMEM((cells_x_y, 128 * tiles), BF16),
            pltpu.VMEM((1024, 128 * tiles), BF16),
            pltpu.VMEM((cells_x_y, 128 * tiles), BF16),
            pltpu.VMEM((1024, cells_x_y), F32),
        ],
        compiler_params=pltpu.CompilerParams(vmem_limit_bytes=48 * MIB),
        cost_estimate=pl.CostEstimate(flops=17 * 10**9, bytes_accessed=2 * MIB, transcendentals=0),
        name="deposit",
    )(table, place)


def write_faces(fields, back_ref, x_low, x_high, y_low, y_high, z_face, x_width, y_width):
    rows = x_width * y_width
    for f, field in enumerate(fields):
        x_low[f * y_width : (f + 1) * y_width, :] = field[0:y_width]
        x_high[f * y_width : (f + 1) * y_width, :] = field[rows - y_width : rows]
        for x in range(x_width):
            at = f * x_width + x
            y_low[at : at + 1, :] = field[x * y_width : x * y_width + 1]
            y_high[at : at + 1, :] = field[(x + 1) * y_width - 1 : (x + 1) * y_width]
    write_z_face(z_face, fields, back_ref)


def source_kernel(
    own_ref, velocity_ref, from_0, from_1, from_2, from_3, back_ref,
    porosity_ref, source_ref, arrivals_ref, x_low, x_high, y_low, y_high, z_face, *, slots,
):
    x_width, y_width = velocity_ref.shape[1], velocity_ref.shape[2]
    rows = x_width * y_width
    got = (from_0, from_1, from_2, from_3)
    hots = []
    for d in range(4):
        ids = lax.broadcasted_iota(jnp.int32, (rows, slots), 0)
        named = got[d][4 * slots : 4 * slots + 1, 0:slots].astype(jnp.int32)
        hots.append(jnp.where(ids == named, 1.0, 0.0))
    hot = jnp.concatenate(hots, axis=1)
    deposit = []
    for f in range(4):
        block = jnp.concatenate([got[d][f * slots : (f + 1) * slots, :] for d in range(4)], axis=0)
        deposit.append(
            own_ref[f]
            + jnp.dot(hot, block, preferred_element_type=F32, precision=lax.Precision.HIGHEST)
        )
    porosity = 1.0 / (1.0 + deposit[3])
    porosity_ref[...] = porosity
    for f in range(3):
        velocity = velocity_ref[f].reshape(rows, 128)
        source_ref[f] = porosity * velocity - source_step * deposit[f]
    for d in range(4):
        at = 4 * slots + 8
        for f in range(3):
            for t in range(arrivals_ref.shape[2] // 128):
                arrivals_ref[d, f : f + 1, t * 128 : (t + 1) * 128] = got[d][at : at + 1, :]
                at += 1
    write_faces([porosity], back_ref, x_low, x_high, y_low, y_high, z_face, x_width, y_width)


def source_part(own, velocity, got, back, slots, movers):
    x_width, y_width = velocity.shape[1], velocity.shape[2]
    rows = x_width * y_width
    vmem = pl.BlockSpec(memory_space=pltpu.VMEM)
    shape = jax.ShapeDtypeStruct
    return pl.pallas_call(
        lambda *refs: source_kernel(*refs, slots=slots),
        in_specs=[vmem] * 6 + [pl.BlockSpec(memory_space=pltpu.SMEM)],
        out_shape=[
            shape((rows, 128), F32),
            shape((3, rows, 128), F32),
            shape((4, 3, movers), F32),
            shape((y_width, 128), F32),
            shape((y_width, 128), F32),
            shape((x_width, 128), F32),
            shape((x_width, 128), F32),
            shape((8, rows), F32),
        ],
        out_specs=[vmem] * 8,
        compiler_params=pltpu.CompilerParams(vmem_limit_bytes=48 * MIB),
        cost_estimate=pl.CostEstimate(flops=10**8, bytes_accessed=2 * MIB, transcendentals=0),
        name="source",
    )(own, velocity, *got, back)


def neighbours(field, below_x, above_x, below_y, above_y, beside, outside, back, x_width, y_width):
    rows = x_width * y_width
    yield jnp.concatenate([below_x, field[0 : rows - y_width]], axis=0)
    yield jnp.concatenate([field[y_width:rows], above_x], axis=0)
    row_in_y = lax.broadcasted_iota(jnp.int32, (rows, 128), 0) % y_width

    def per_x(edge):
        return jnp.broadcast_to(edge[:, None, :], (x_width, y_width, 128)).reshape(rows, 128)

    yield jnp.where(row_in_y == 0, per_x(below_y), pltpu.roll(field, 1, axis=0))
    yield jnp.where(row_in_y == y_width - 1, per_x(above_y), pltpu.roll(field, rows - 1, axis=0))
    lane = lax.broadcasted_iota(jnp.int32, (rows, 128), 1)
    partner = jnp.broadcast_to(beside, (128, rows)).T
    wall = jnp.full((rows, 128), outside, F32)
    yield jnp.where(lane == 0, jnp.where(back, partner, wall), pltpu.roll(field, 1, axis=1))
    yield jnp.where(lane == 127, jnp.where(back, wall, partner), pltpu.roll(field, 127, axis=1))


def sweep_kernel(
    u_ref, source_ref, porosity_ref, px_low, px_high, py_low, py_high, p_beside,
    ux_low, ux_high, uy_low, uy_high, u_beside, back_ref, *outs, starts, x_width, y_width,
):
    rows = x_width * y_width
    back = back_ref[0] > 0
    porosity = porosity_ref[...]
    weights = [
        0.5 * (porosity + near)
        for near in neighbours(
            porosity, px_low[...], px_high[...], py_low[...], py_high[...], p_beside[0:1, :],
            1.0, back, x_width, y_width,
        )
    ]
    weight_sum = weights[0]
    for weight in weights[1:]:
        weight_sum = weight_sum + weight
    scale = 1.0 / (porosity + coupling * weight_sum)
    fields = []
    x_at, y_at = starts
    for f in range(3):
        field = u_ref[f].reshape(rows, 128)
        flux = None
        edge_x = slice(x_at + f * y_width, x_at + (f + 1) * y_width)
        edge_y = slice(y_at + f * x_width, y_at + (f + 1) * x_width)
        nears = neighbours(
            field, ux_low[edge_x, :], ux_high[edge_x, :], uy_low[edge_y, :], uy_high[edge_y, :],
            u_beside[f : f + 1, :], 0.0, back, x_width, y_width,
        )
        for weight, near in zip(weights, nears):
            flux = weight * near if flux is None else flux + weight * near
        fields.append((source_ref[f] + coupling * flux) * scale)
        outs[0][f] = fields[-1].reshape(outs[0].shape[1:])
    if len(outs) > 1:
        write_faces(fields, back_ref, *outs[1:], x_width, y_width)


def sweep_part(u, source, porosity, porosity_faces, u_faces, back, starts, x_width, y_width, last):
    rows = x_width * y_width
    vmem = pl.BlockSpec(memory_space=pltpu.VMEM)
    shape = jax.ShapeDtypeStruct
    outs = [shape((3, x_width, y_width, 128), F32)]
    if not last:
        outs += [
            shape((3 * y_width, 128), F32),
            shape((3 * y_width, 128), F32),
            shape((3 * x_width, 128), F32),
            shape((3 * x_width, 128), F32),
            shape((8, rows), F32),
        ]
    return pl.pallas_call(
        lambda *refs: sweep_kernel(*refs, starts=starts, x_width=x_width, y_width=y_width),
        in_specs=[vmem] * 13 + [pl.BlockSpec(memory_space=pltpu.SMEM)],
        out_shape=outs,
        out_specs=[vmem] * len(outs),
        compiler_params=pltpu.CompilerParams(vmem_limit_bytes=48 * MIB),
        cost_estimate=pl.CostEstimate(flops=10**7, bytes_accessed=2 * MIB, transcendentals=0),
        name="sweep",
    )(u, source, porosity, *porosity_faces, *u_faces, back)


def moved_along(value, axis, steps):
    count = lax.axis_size(axis)
    return lax.ppermute(value, axis, [(i, (i + steps) % count) for i in range(count)])


def swap_faces(x_low, x_high, y_low, y_high, z_face):
    above_x = moved_along(x_low, "gx", -1)
    below_x = moved_along(x_high, "gx", 1)
    above_y = moved_along(y_low, "gy", -1)
    below_y = moved_along(y_high, "gy", 1)
    return below_x, above_x, below_y, above_y, moved_along(z_face, "gz", 1)


def body(
    velocity, fibre_vel, fluid_vel, fibre_props, fibre_row, fibre_height, migrant_list, migrant_slot, side_rows,
):
    x_width, y_width = velocity.shape[1], velocity.shape[2]
    slots, movers = side_rows.shape[1], migrant_list.shape[1]
    back = lax.axis_index("gz").astype(jnp.int32).reshape(1)
    kept, table, place, *faces = fibre_part(
        fibre_vel, fluid_vel, fibre_props, fibre_row.reshape(-1, 128), fibre_height.reshape(-1, 128),
        migrant_list, migrant_slot, side_rows, velocity, back,
    )
    below_x, above_x, below_y, above_y, beside = u_faces = swap_faces(*faces)
    own = deposit_part(table, place, x_width * y_width)
    porosity, source, arrivals, *faces = source_part(
        own, velocity, (above_x, below_x, above_y, below_y), back, slots, movers
    )
    porosity_faces = swap_faces(*faces)
    base = 4 * slots + 8 + 3 * (movers // 128)
    starts = (base, base)
    u = velocity
    for step in range(SWEEPS):
        last = step == SWEEPS - 1
        u, *faces = sweep_part(
            u, source, porosity, porosity_faces, u_faces, back, starts, x_width, y_width, last
        )
        if not last:
            u_faces = swap_faces(*faces)
            starts = (0, 0)
    return u, kept, arrivals


def solution(mesh):
    by_device = P(None, ("gx", "gy", "gz"))
    one_row = P(("gx", "gy", "gz"))
    grid = P(None, "gx", "gy", "gz")
    return jax.shard_map(
        body,
        mesh=mesh,
        in_specs=(grid, by_device, by_device, by_device, one_row, one_row, by_device, by_device, by_device),
        out_specs=(grid, by_device, P(None, None, ("gx", "gy", "gz"))),
        check_vma=False,
    )
```

```python
import jax
import jax.numpy as jnp
from jax import lax
from jax.experimental import pallas as pl
from jax.experimental.pallas import tpu as pltpu
from jax.sharding import PartitionSpec as P

F32 = jnp.float32
BF16 = jnp.bfloat16
NT = (((1,), (1,)), ((), ()))
drag_step = 0.25
source_step = 1.0
coupling = 1.0
SWEEPS = 3
TILE = 8
LANES = 128
MIB = 2**20


def two_parts(value):
    high = value.astype(BF16)
    return high, (value - high.astype(F32)).astype(BF16)


def one_hot(index_row, count):
    ids = lax.broadcasted_iota(jnp.int32, (count, index_row.shape[1]), 0)
    return jnp.where(ids == index_row, 1.0, 0.0).astype(BF16)


def ordered(value, after):
    return lax.optimization_barrier((value, after))[0]


VMEM = pl.BlockSpec(memory_space=pltpu.VMEM)
SMEM = pl.BlockSpec(memory_space=pltpu.SMEM)
HBM = pl.BlockSpec(memory_space=pltpu.HBM)


def call(kernel, outs, ins, name, flops, in_specs=None, scratch=(), vmem=48):
    return pl.pallas_call(
        kernel,
        out_shape=[jax.ShapeDtypeStruct(shape, F32) for shape in outs],
        in_specs=in_specs or [VMEM] * len(ins),
        out_specs=[VMEM] * len(outs),
        scratch_shapes=list(scratch),
        compiler_params=pltpu.CompilerParams(vmem_limit_bytes=vmem * MIB),
        cost_estimate=pl.CostEstimate(flops=flops, bytes_accessed=2 * MIB, transcendentals=0),
        name=name,
    )(*ins)


def height_pack(fields, back_ref, out_ref):
    back = back_ref[0] > 0
    for f, field in enumerate(fields):
        turned = field.T
        out_ref[TILE * f : TILE * (f + 1), :] = jnp.where(
            back, turned[0:TILE, :], turned[LANES - TILE : LANES, :]
        )


def beside_rows(got):
    rest = jnp.zeros((LANES - got.shape[0], got.shape[1]), F32)
    return jnp.concatenate([got, rest], axis=0).T


def row_ids(width=LANES):
    return lax.broadcasted_iota(jnp.int32, (TILE, width), 0)


def y_pack(fields, x_width, y_width, low_ref, high_ref, base):
    half = x_width // 2
    ids = row_ids()
    for g, field in enumerate(fields):
        for p in range(half):
            at = base + (g * half + p) * TILE
            near, far = p * y_width, (p + half) * y_width
            low_ref[at : at + TILE, :] = jnp.where(
                ids < 4, field[near : near + TILE], pltpu.roll(field[far : far + TILE], 4, axis=0)
            )
            near, far = near + y_width - TILE, far + y_width - TILE
            high_ref[at : at + TILE, :] = jnp.where(
                ids < 4, pltpu.roll(field[far : far + TILE], 4, axis=0), field[near : near + TILE]
            )


def y_halo(above_ref, below_ref, base, g, p, x_width):
    half = x_width // 2
    at = base + (g * half + p % half) * TILE
    above, below = above_ref[at : at + TILE, :], below_ref[at : at + TILE, :]
    if p >= half:
        above, below = pltpu.roll(above, 4, axis=0), pltpu.roll(below, 4, axis=0)
    return jnp.where(row_ids() < 4, above, below)


def x_pack(fields, depths, halo, x_width, y_width, low_ref, high_ref, base):
    at = base
    for g, field in enumerate(fields):
        for k in range(depths[g]):
            for ref, plane in ((low_ref, k), (high_ref, x_width - depths[g] + k)):
                ref[at : at + y_width, :] = field[plane * y_width : (plane + 1) * y_width]
                ref[at + y_width : at + y_width + TILE, :] = halo(g, plane)
            at += y_width + TILE


VELOCITY_DEPTHS = (3, 3, 3, 2)
DEPOSIT_DEPTHS = (2, 2, 2, 3, 2)


def flat(ref, f):
    return ref[f].reshape(-1, LANES)


def heights_kernel(velocity_ref, back_ref, out_ref):
    height_pack([flat(velocity_ref, f) for f in range(3)], back_ref, out_ref)


def fibre_kernel(
    vel_hbm, fluid_hbm, props_hbm, row_hbm, height_hbm, list_hbm, slot_hbm, ids_ref,
    kept_ref, table_ref, place_ref, pack_0, pack_1, pack_2, pack_3,
    vel_ref, fluid_ref, props_ref, row_ref, height_ref, list_ref, slot_ref, hot_ref, stay_ref, arrived,
):
    loads = [
        pltpu.make_async_copy(source, target, arrived.at[k])
        for k, (source, target) in enumerate(
            (
                (list_hbm, list_ref), (row_hbm, row_ref), (vel_hbm, vel_ref), (fluid_hbm, fluid_ref),
                (props_hbm, props_ref), (height_hbm, height_ref), (slot_hbm, slot_ref),
            )
        )
    ]
    for load in loads:
        load.start()
    loads[0].wait()
    tiles = row_ref.shape[0]
    movers = list_ref.shape[1]
    packs = (pack_0, pack_1, pack_2, pack_3)
    slots = ids_ref.shape[1]
    hits = jnp.zeros((tiles, 128), F32)
    for d in range(4):
        named = list_ref[d : d + 1, :]
        tile_hot = one_hot(named // 128, tiles)
        hot_ref[d, 0:tiles, :] = tile_hot
        hot_ref[d, tiles : 2 * tiles, :] = tile_hot
        hits += lax.dot_general(
            tile_hot, one_hot(named % 128, 128), NT, preferred_element_type=F32
        )
    for load in loads[1:]:
        load.wait()
    stay_ref[...] = 1.0 - hits
    place_ref[...] = jnp.where(hits > 0.5, -1.0, row_ref[...].astype(F32))

    def terms(block, _):
        for inner in range(8):
            tile = block * 8 + inner
            lanes = pl.ds(pl.multiple_of(tile * 128, 128), 128)
            vel = vel_ref[:, lanes]
            volume = props_ref[0:1, lanes]
            force = props_ref[1:2, lanes] * (fluid_ref[:, lanes] - vel)
            moved = vel + drag_step * force / volume
            kept_ref[:, lanes] = moved * stay_ref[pl.ds(tile, 1), :]
            table_ref[pl.ds(tile * 8, 3), :] = force
            table_ref[pl.ds(tile * 8 + 3, 1), :] = volume
            table_ref[pl.ds(tile * 8 + 4, 3), :] = moved
            table_ref[pl.ds(tile * 8 + 7, 1), :] = height_ref[pl.ds(tile, 1), :].astype(F32)
        return 0

    lax.fori_loop(0, tiles // 8, terms, 0)
    tables = []
    for f in range(8):
        field = table_ref[pl.ds(f, tiles, stride=8), :].T
        high, low = two_parts(field)
        tables.append(jnp.concatenate([high, low], axis=1))
    lane_ids = lax.broadcasted_iota(jnp.int32, (128, movers), 0)
    for d in range(4):
        lane_hit = lane_ids == list_ref[d : d + 1, :] % 128
        picked = []
        for f in range(8):
            columns = jnp.dot(tables[f], hot_ref[d], preferred_element_type=F32)
            picked.append(jnp.sum(jnp.where(lane_hit, columns, 0.0), axis=0, keepdims=True))
        at_height = lane_ids == picked[7].astype(jnp.int32)
        slot_hot = one_hot(slot_ref[d : d + 1, :], slots)
        for f in range(4):
            high, low = two_parts(picked[f])
            spread = jnp.concatenate(
                [
                    jnp.where(at_height, high.astype(F32), 0.0).astype(BF16),
                    jnp.where(at_height, low.astype(F32), 0.0).astype(BF16),
                ],
                axis=0,
            )
            rows = lax.dot_general(slot_hot, spread, NT, preferred_element_type=F32)
            packs[d][f * slots : (f + 1) * slots, :] = rows[:, 0:128] + rows[:, 128:256]
        at = 4 * slots
        packs[d][at : at + 8, :] = jnp.zeros((8, 128), F32)
        packs[d][at : at + 1, 0:slots] = ids_ref[d : d + 1, :].astype(F32)
        at += 8
        for f in range(3):
            for t in range(movers // 128):
                packs[d][at : at + 1, :] = picked[4 + f][:, t * 128 : (t + 1) * 128]
                at += 1


def fibre_part(vel, fluid, props, row, height, lists, slots, ids):
    tiles = row.shape[0]
    movers = lists.shape[1]
    pack = (4 * ids.shape[1] + 8 + 3 * (movers // 128), 128)
    ins = tuple(
        pltpu.with_memory_space_constraint(value, pltpu.HBM)
        for value in (vel, fluid, props, row, height, lists, slots)
    ) + (ids,)
    return call(
        fibre_kernel,
        [vel.shape, (tiles * 8, 128), (tiles, 128)] + [pack] * 4,
        ins,
        "fibre_terms",
        10**9,
        [HBM] * 7 + [VMEM],
        [pltpu.VMEM(value.shape, value.dtype) for value in ins[:7]]
        + [pltpu.VMEM((4, 2 * tiles, movers), BF16), pltpu.VMEM((tiles, 128), F32), pltpu.SemaphoreType.DMA((7,))],
    )


def spread_tiles(table_ref, place_ref, values_ref, rows_ref, tiles):
    ids = lax.broadcasted_iota(jnp.int32, (16, 128), 0).astype(F32).astype(BF16)
    zero = jnp.zeros((16, 128), BF16)
    one = jnp.ones((16, 128), BF16)
    row_groups = rows_ref.shape[0] // 16
    for c in range(tiles):
        lanes = slice(c * 128, (c + 1) * 128)
        place = jnp.broadcast_to(place_ref[c : c + 1, :], (16, 128)).astype(BF16)
        for i in range(row_groups):
            rows_ref[16 * i : 16 * i + 16, lanes] = jnp.where(ids + BF16(16 * i) == place, one, zero)
        height = jnp.broadcast_to(table_ref[8 * c + 7 : 8 * c + 8, :], (16, 128)).astype(BF16)
        parts = []
        for f in range(4):
            parts.extend(two_parts(jnp.broadcast_to(table_ref[8 * c + f : 8 * c + f + 1, :], (16, 128))))
        for i in range(8):
            hit = ids + BF16(16 * i) == height
            for p in range(8):
                at = 128 * p + 16 * i
                values_ref[at : at + 16, lanes] = jnp.where(hit, parts[p], zero)


def deposit_kernel(table_ref, place_ref, out_ref, values_a, rows_a, values_b, rows_b, total, *, tiles, first):
    steps = place_ref.shape[0] // tiles
    total[...] = jnp.zeros_like(total)

    def fill(step, values, rows):
        spread_tiles(
            table_ref.at[pl.ds(pl.multiple_of(step * 8 * tiles, 8 * tiles), 8 * tiles), :],
            place_ref.at[pl.ds(pl.multiple_of(step * tiles, 8), tiles), :],
            values, rows, tiles,
        )

    fill(0, values_a, rows_a)

    def pair(j, _):
        part = lax.dot_general(values_a[...], rows_a[...], NT, preferred_element_type=F32)
        fill(2 * j + 1, values_b, rows_b)
        total[...] += part
        part = lax.dot_general(values_b[...], rows_b[...], NT, preferred_element_type=F32)
        fill(lax.rem(2 * j + 2, steps), values_a, rows_a)
        total[...] += part
        return 0

    lax.fori_loop(0, steps // 2, pair, 0)
    for f in range(4):
        at = 256 * f
        out_ref[128 * f : 128 * f + 128, :] = total[at : at + 128, :] + total[at + 128 : at + 256, :]


def deposit_part(table, place, cells_x_y, part, parts):
    tiles = 8
    count = place.shape[0] // parts
    return pl.pallas_call(
        lambda *refs: deposit_kernel(*refs, tiles=tiles, first=part * count),
        grid=(1,),
        in_specs=[
            pl.BlockSpec((8 * count, 128), lambda i: (part, 0)),
            pl.BlockSpec((count, 128), lambda i: (part, 0)),
        ],
        out_specs=pl.BlockSpec((512, cells_x_y), lambda i: (0, 0)),
        out_shape=jax.ShapeDtypeStruct((512, cells_x_y), F32),
        scratch_shapes=[
            pltpu.VMEM((1024, 128 * tiles), BF16),
            pltpu.VMEM((cells_x_y, 128 * tiles), BF16),
            pltpu.VMEM((1024, 128 * tiles), BF16),
            pltpu.VMEM((cells_x_y, 128 * tiles), BF16),
            pltpu.VMEM((1024, cells_x_y), F32),
        ],
        compiler_params=pltpu.CompilerParams(vmem_limit_bytes=48 * MIB),
        cost_estimate=pl.CostEstimate(
            flops=17 * 10**9 // parts, bytes_accessed=MIB, transcendentals=0
        ),
        name="deposit",
    )(table, place)


def velocity_y_kernel(velocity_ref, heights_ref, mig_low, mig_high, beside_ref, low_ref, high_ref):
    x_width, y_width = velocity_ref.shape[1], velocity_ref.shape[2]
    base = mig_low.shape[0]
    low_ref[0:base, :] = mig_low[...]
    high_ref[0:base, :] = mig_high[...]
    beside = beside_rows(heights_ref[...])
    beside_ref[...] = beside
    fields = [flat(velocity_ref, f) for f in range(3)] + [beside]
    y_pack(fields, x_width, y_width, low_ref, high_ref, base)


def velocity_x_kernel(velocity_ref, beside_ref, above_ref, below_ref, mig_low, mig_high, low_ref, high_ref):
    x_width, y_width = velocity_ref.shape[1], velocity_ref.shape[2]
    base = mig_low.shape[0]
    low_ref[0:base, :] = mig_low[...]
    high_ref[0:base, :] = mig_high[...]
    fields = [flat(velocity_ref, f) for f in range(3)] + [beside_ref[...]]

    def halo(g, p):
        return y_halo(above_ref, below_ref, base, g, p, x_width)

    x_pack(fields, VELOCITY_DEPTHS, halo, x_width, y_width, low_ref, high_ref, base)


def total_kernel(*refs, slots, parts):
    parts_ref = refs[:parts]
    got = refs[parts : parts + 4]
    back_ref = refs[parts + 4]
    deposit_ref, arrivals_ref, heights_ref = refs[parts + 5 :]
    rows = deposit_ref.shape[1]
    hots = []
    for d in range(4):
        ids = lax.broadcasted_iota(jnp.int32, (rows, slots), 0)
        named = got[d][4 * slots : 4 * slots + 1, 0:slots].astype(jnp.int32)
        hots.append(jnp.where(ids == named, 1.0, 0.0))
    hot = jnp.concatenate(hots, axis=1)
    deposit = []
    for f in range(4):
        at = 128 * f
        own = parts_ref[0][at : at + 128, :]
        for ref in parts_ref[1:]:
            own = own + ref[at : at + 128, :]
        block = jnp.concatenate([got[d][f * slots : (f + 1) * slots, :] for d in range(4)], axis=0)
        deposit.append(
            own.T
            + jnp.dot(hot, block, preferred_element_type=F32, precision=lax.Precision.HIGHEST)
        )
        deposit_ref[f] = deposit[f]
    height_pack(deposit, back_ref, heights_ref)
    for d in range(4):
        at = 4 * slots + 8
        for f in range(3):
            for t in range(arrivals_ref.shape[2] // 128):
                arrivals_ref[d, f : f + 1, t * 128 : (t + 1) * 128] = got[d][at : at + 1, :]
                at += 1


def deposit_y_kernel(deposit_ref, heights_ref, beside_ref, low_ref, high_ref, *, x_width, y_width):
    beside = beside_rows(heights_ref[...])
    beside_ref[...] = beside
    y_pack([deposit_ref[f] for f in range(4)] + [beside], x_width, y_width, low_ref, high_ref, 0)


def deposit_x_kernel(deposit_ref, beside_ref, above_ref, below_ref, low_ref, high_ref, *, x_width, y_width):
    def halo(g, p):
        return y_halo(above_ref, below_ref, 0, g, p, x_width)

    fields = [deposit_ref[f] for f in range(4)] + [beside_ref[...]]
    x_pack(fields, DEPOSIT_DEPTHS, halo, x_width, y_width, low_ref, high_ref, 0)


def sweeps_kernel(
    velocity_ref, v_beside, v_above_y, v_below_y, v_above_x, v_below_x,
    deposit_ref, d_beside, d_above_y, d_below_y, d_above_x, d_below_x, back_ref,
    out_ref, u_a, u_b, source, porosity, w_x, w_y_low, w_y_high, w_z_low, w_z_high, scale,
    *, base,
):
    x_width, y_width = velocity_ref.shape[1], velocity_ref.shape[2]
    reach = SWEEPS
    planes = x_width + 2 * reach
    tall = y_width + TILE
    back = back_ref[0] > 0
    lane = lax.broadcasted_iota(jnp.int32, (tall, LANES), 1)
    partner_at = jnp.where(back, LANES - reach, 0)
    partner = (lane >= partner_at) & (lane < partner_at + reach)
    nothing = jnp.zeros((tall, LANES), F32)

    def plane_of(own, above_y, below_y, above_x, below_x, depths, start, g, plane):
        x = plane - reach
        before = start + tall * sum(depths[:g])
        if x < 0:
            k = x + depths[g]
            if k < 0:
                return nothing
            return below_x[before + k * tall : before + (k + 1) * tall, :]
        if x >= x_width:
            k = x - x_width
            if k >= depths[g]:
                return nothing
            return above_x[before + k * tall : before + (k + 1) * tall, :]
        return jnp.concatenate([own(g, x), y_halo(above_y, below_y, start_y[start > 0], g, x, x_width)], axis=0)

    start_y = {True: base, False: 0}

    def beside_of(packed, f):
        shift = jnp.where(back, LANES - TILE - TILE * f, (LANES - TILE * f) % LANES)
        return jnp.where(partner, pltpu.roll(packed, shift, axis=1), 0.0)

    def v_own(g, x):
        return velocity_ref[g, x] if g < 3 else v_beside[x * y_width : (x + 1) * y_width, :]

    def d_own(g, x):
        ref = deposit_ref.at[g] if g < 4 else d_beside
        return ref[x * y_width : (x + 1) * y_width, :]

    for p in range(planes):
        v_args = (v_own, v_above_y, v_below_y, v_above_x, v_below_x, VELOCITY_DEPTHS, base)
        d_args = (d_own, d_above_y, d_below_y, d_above_x, d_below_x, DEPOSIT_DEPTHS, 0)
        v_packed, d_packed = plane_of(*v_args, 3, p), plane_of(*d_args, 4, p)
        por = jnp.concatenate(
            [1.0 / (1.0 + plane_of(*d_args, 3, p)), 1.0 / (1.0 + beside_of(d_packed, 3))], axis=1
        )
        porosity[p] = por
        for f in range(3):
            u = jnp.concatenate([plane_of(*v_args, f, p), beside_of(v_packed, f)], axis=1)
            u_a[f, p] = u
            if 0 < p < planes - 1:
                drag = jnp.concatenate([plane_of(*d_args, f, p), beside_of(d_packed, f)], axis=1)
                source[f, p] = por * u - source_step * drag

    def weights(p, _):
        por = porosity[p]
        low, high = 0.5 * (por + porosity[p - 1]), 0.5 * (por + porosity[p + 1])
        w_x[p - 1] = low
        w_x[p] = high
        total = low + high
        for ref, axis, shift in (
            (w_y_low, 0, 1), (w_y_high, 0, tall - 1), (w_z_low, 1, 1), (w_z_high, 1, 2 * LANES - 1),
        ):
            weight = 0.5 * (por + pltpu.roll(por, shift, axis=axis))
            ref[p] = weight
            total = total + weight
        scale[p] = 1.0 / (por + coupling * total)
        return 0

    lax.fori_loop(1, planes - 1, weights, 0)
    inside = jnp.concatenate([jnp.full((tall, LANES), 1.0, F32), jnp.where(partner, 1.0, 0.0)], axis=1)
    for step in range(SWEEPS):
        old, new = ((u_a, u_b), (u_b, u_a))[step % 2]

        def relax(p, _):
            for f in range(3):
                u = old[f, p]
                flux = w_x[p - 1] * old[f, p - 1] + w_x[p] * old[f, p + 1]
                flux = flux + w_y_low[p] * pltpu.roll(u, 1, axis=0)
                flux = flux + w_y_high[p] * pltpu.roll(u, tall - 1, axis=0)
                flux = flux + w_z_low[p] * pltpu.roll(u, 1, axis=1)
                flux = flux + w_z_high[p] * pltpu.roll(u, 2 * LANES - 1, axis=1)
                result = (source[f, p] + coupling * flux) * scale[p]
                if step < SWEEPS - 1:
                    new[f, p] = result * inside
                else:
                    out_ref[f, p - reach] = result[0:y_width, 0:LANES]
            return 0

        lax.fori_loop(step + 1, planes - 1 - step, relax, 0)


def moved_along(value, axis, steps):
    count = lax.axis_size(axis)
    return lax.ppermute(value, axis, [(i, (i + steps) % count) for i in range(count)])


def body(
    velocity, fibre_vel, fluid_vel, fibre_props, fibre_row, fibre_height, migrant_list, migrant_slot, side_rows,
):
    x_width, y_width = velocity.shape[1], velocity.shape[2]
    rows = x_width * y_width
    tall = y_width + TILE
    slots, movers = side_rows.shape[1], migrant_list.shape[1]
    back = lax.axis_index("gz").astype(jnp.int32).reshape(1)
    heights, = call(heights_kernel, [(3 * TILE, rows)], (velocity, back), "velocity_heights", 10**7, [VMEM, SMEM])
    v_heights = moved_along(heights, "gz", 1)
    kept, table, place, *migs = fibre_part(
        fibre_vel, fluid_vel, fibre_props, fibre_row.reshape(-1, 128), fibre_height.reshape(-1, 128),
        migrant_list, migrant_slot, side_rows,
    )
    base = migs[0].shape[0]
    y_rows = base + 4 * rows // y_width * TILE // 2
    v_beside, low, high = call(
        velocity_y_kernel, [(rows, 128), (y_rows, 128), (y_rows, 128)], (velocity, v_heights, migs[2], migs[3]),
        "velocity_y_rows", 10**7,
    )
    PARTS = 4
    v_above_y = moved_along(low, "gy", -1)
    part_0 = deposit_part(table, ordered(place, low), rows, 0, PARTS)
    v_below_y = moved_along(ordered(high, part_0), "gy", 1)
    part_1 = deposit_part(table, ordered(place, (v_above_y, part_0)), rows, 1, PARTS)
    x_rows = base + tall * sum(VELOCITY_DEPTHS)
    low, high = call(
        velocity_x_kernel, [(x_rows, 128), (x_rows, 128)],
        (velocity, v_beside, v_above_y, ordered(v_below_y, part_1), migs[0], migs[1]), "velocity_x_planes", 10**7,
    )
    v_above_x = moved_along(low, "gx", -1)
    part_2 = deposit_part(table, ordered(place, (low, part_1)), rows, 2, PARTS)
    v_below_x = moved_along(ordered(high, part_2), "gx", 1)
    part_3 = deposit_part(table, ordered(place, (v_above_x, part_2)), rows, 3, PARTS)
    deposit, arrivals, heights = call(
        lambda *refs: total_kernel(*refs, slots=slots, parts=PARTS),
        [(4, rows, 128), (4, 3, movers), (4 * TILE, rows)],
        (part_0, part_1, part_2, part_3, v_above_x, v_below_x, v_above_y, v_below_y, back),
        "deposit_total", 10**7, [VMEM] * 8 + [SMEM],
    )
    d_heights = moved_along(heights, "gz", 1)
    y_rows = 5 * rows // y_width * TILE // 2
    d_beside, low, high = call(
        lambda *refs: deposit_y_kernel(*refs, x_width=x_width, y_width=y_width),
        [(rows, 128), (y_rows, 128), (y_rows, 128)], (deposit, d_heights), "deposit_y_rows", 10**7,
    )
    d_above_y = moved_along(low, "gy", -1)
    d_below_y = moved_along(high, "gy", 1)
    x_rows = tall * sum(DEPOSIT_DEPTHS)
    low, high = call(
        lambda *refs: deposit_x_kernel(*refs, x_width=x_width, y_width=y_width),
        [(x_rows, 128), (x_rows, 128)], (deposit, d_beside, d_above_y, d_below_y), "deposit_x_planes", 10**7,
    )
    d_above_x = moved_along(low, "gx", -1)
    d_below_x = moved_along(high, "gx", 1)
    planes = x_width + 2 * SWEEPS
    field = pltpu.VMEM((planes, tall, 256), F32)
    three = pltpu.VMEM((3, planes, tall, 256), F32)
    u, = call(
        lambda *refs: sweeps_kernel(*refs, base=base),
        [velocity.shape],
        (
            velocity, v_beside, v_above_y, v_below_y, v_above_x, v_below_x,
            deposit, d_beside, d_above_y, d_below_y, d_above_x, d_below_x, back,
        ),
        "sweeps", 10**8, [VMEM] * 12 + [SMEM], [three, three, three] + [field] * 7,
    )
    return u, kept, arrivals


def solution(mesh):
    by_device = P(None, ("gx", "gy", "gz"))
    one_row = P(("gx", "gy", "gz"))
    grid = P(None, "gx", "gy", "gz")
    return jax.shard_map(
        body,
        mesh=mesh,
        in_specs=(grid, by_device, by_device, by_device, one_row, one_row, by_device, by_device, by_device),
        out_specs=(grid, by_device, P(None, None, ("gx", "gy", "gz"))),
        check_vma=False,
    )
```

```python
import jax
import jax.numpy as jnp
from jax import lax
from jax.experimental import pallas as pl
from jax.experimental.pallas import tpu as pltpu
from jax.sharding import PartitionSpec as P

F32 = jnp.float32
BF16 = jnp.bfloat16
NT = (((1,), (1,)), ((), ()))
drag_step = 0.25
source_step = 1.0
coupling = 1.0
SWEEPS = 3
TILE = 8
DEPOSIT_TILES = 8
DEPOSIT_COUNTS = (96, 128, 32)
LANES = 128
MIB = 2**20


def two_parts(value):
    high = value.astype(BF16)
    return high, (value - high.astype(F32)).astype(BF16)


def one_hot(index_row, count):
    ids = lax.broadcasted_iota(jnp.int32, (count, index_row.shape[1]), 0)
    return jnp.where(ids == index_row, 1.0, 0.0).astype(BF16)


def ordered(value, after):
    return lax.optimization_barrier((value, after))[0]


VMEM = pl.BlockSpec(memory_space=pltpu.VMEM)
SMEM = pl.BlockSpec(memory_space=pltpu.SMEM)
HBM = pl.BlockSpec(memory_space=pltpu.HBM)


def call(kernel, outs, ins, name, flops, in_specs=None, scratch=(), vmem=48):
    return pl.pallas_call(
        kernel,
        out_shape=[jax.ShapeDtypeStruct(shape, F32) for shape in outs],
        in_specs=in_specs or [VMEM] * len(ins),
        out_specs=[VMEM] * len(outs),
        scratch_shapes=list(scratch),
        compiler_params=pltpu.CompilerParams(vmem_limit_bytes=vmem * MIB),
        cost_estimate=pl.CostEstimate(flops=flops, bytes_accessed=2 * MIB, transcendentals=0),
        name=name,
    )(*ins)


def height_pack(fields, back_ref, out_ref):
    back = back_ref[0] > 0
    for f, field in enumerate(fields):
        turned = field.T
        out_ref[TILE * f : TILE * (f + 1), :] = jnp.where(
            back, turned[0:TILE, :], turned[LANES - TILE : LANES, :]
        )


def beside_rows(got):
    rest = jnp.zeros((LANES - got.shape[0], got.shape[1]), F32)
    return jnp.concatenate([got, rest], axis=0).T


def row_ids(width=LANES):
    return lax.broadcasted_iota(jnp.int32, (TILE, width), 0)


def y_pack(fields, x_width, y_width, low_ref, high_ref, base):
    half = x_width // 2
    ids = row_ids()
    for g, field in enumerate(fields):
        for p in range(half):
            at = base + (g * half + p) * TILE
            near, far = p * y_width, (p + half) * y_width
            low_ref[at : at + TILE, :] = jnp.where(
                ids < 4, field[near : near + TILE], pltpu.roll(field[far : far + TILE], 4, axis=0)
            )
            near, far = near + y_width - TILE, far + y_width - TILE
            high_ref[at : at + TILE, :] = jnp.where(
                ids < 4, pltpu.roll(field[far : far + TILE], 4, axis=0), field[near : near + TILE]
            )


def y_halo(above_ref, below_ref, base, g, p, x_width):
    half = x_width // 2
    at = base + (g * half + p % half) * TILE
    above, below = above_ref[at : at + TILE, :], below_ref[at : at + TILE, :]
    if p >= half:
        above, below = pltpu.roll(above, 4, axis=0), pltpu.roll(below, 4, axis=0)
    return jnp.where(row_ids() < 4, above, below)


def x_pack(fields, depths, halo, x_width, y_width, low_ref, high_ref, base):
    at = base
    for g, field in enumerate(fields):
        for k in range(depths[g]):
            for ref, plane in ((low_ref, k), (high_ref, x_width - depths[g] + k)):
                ref[at : at + y_width, :] = field[plane * y_width : (plane + 1) * y_width]
                ref[at + y_width : at + y_width + TILE, :] = halo(g, plane)
            at += y_width + TILE


VELOCITY_DEPTHS = (3, 3, 3, 2)
DEPOSIT_DEPTHS = (2, 2, 2, 3, 2)


def flat(ref, f):
    return ref[f].reshape(-1, LANES)


def heights_kernel(velocity_ref, back_ref, out_ref):
    height_pack([flat(velocity_ref, f) for f in range(3)], back_ref, out_ref)


def gather_table(table_ref, tiles, fields):
    stack = []
    for f in fields:
        high, low = two_parts(table_ref[pl.ds(f, tiles, stride=8), :].T)
        stack.append(jnp.concatenate([high, low], axis=1))
    return jnp.concatenate(stack, axis=0)


def gathered(tables, tile_hot, named):
    lane_hit = lax.broadcasted_iota(jnp.int32, (128, named.shape[1]), 0) == named % 128
    columns = jnp.dot(tables, tile_hot, preferred_element_type=F32)
    return [
        jnp.sum(jnp.where(lane_hit, columns[at : at + 128, :], 0.0), axis=0, keepdims=True)
        for at in range(0, columns.shape[0], 128)
    ]


def movers_kernel(table_ref, list_ref, place_ref, first_ref, second_ref, *kept, first):
    tiles = place_ref.shape[0]
    tables = gather_table(table_ref, tiles, (4, 5, 6))
    for d, out_ref in enumerate((first_ref, second_ref)):
        named = list_ref[first + d : first + d + 1, :]
        tile_hot = one_hot(named // 128, tiles)
        picked = gathered(tables, jnp.concatenate([tile_hot, tile_hot], axis=0), named)
        at = 0
        for f in range(3):
            for t in range(named.shape[1] // 128):
                out_ref[at : at + 1, :] = picked[f][:, t * 128 : (t + 1) * 128]
                at += 1
    if kept:

        def keep(block, _):
            for inner in range(8):
                tile = block * 8 + inner
                lanes = pl.ds(pl.multiple_of(tile * 128, 128), 128)
                stay = jnp.where(place_ref[pl.ds(tile, 1), :] < 0.0, 0.0, 1.0)
                kept[0][:, lanes] = table_ref[pl.ds(tile * 8 + 4, 3), :] * stay
            return 0

        lax.fori_loop(0, tiles // 8, keep, 0)


def fibre_kernel(
    vel_hbm, fluid_hbm, props_hbm, row_hbm, height_hbm, list_hbm, slot_hbm, ids_hbm,
    table_ref, place_ref, pack_0, pack_1, pack_2, pack_3,
    vel_ref, fluid_ref, props_ref, row_ref, height_ref, list_ref, slot_ref, ids_ref, hot_ref, arrived,
):
    loads = [
        pltpu.make_async_copy(source, target, arrived.at[k])
        for k, (source, target) in enumerate(
            (
                (list_hbm, list_ref), (row_hbm, row_ref), (vel_hbm, vel_ref), (fluid_hbm, fluid_ref),
                (props_hbm, props_ref), (height_hbm, height_ref), (slot_hbm, slot_ref),
                (ids_hbm, ids_ref),
            )
        )
    ]
    for load in loads:
        load.start()
    loads[0].wait()
    tiles = row_ref.shape[0]
    movers = list_ref.shape[1]
    packs = (pack_0, pack_1, pack_2, pack_3)
    slots = ids_ref.shape[1]
    hits = jnp.zeros((tiles, 128), F32)
    for d in range(4):
        named = list_ref[d : d + 1, :]
        tile_hot = one_hot(named // 128, tiles)
        hot_ref[d, 0:tiles, :] = tile_hot
        hot_ref[d, tiles : 2 * tiles, :] = tile_hot
        hits += lax.dot_general(
            tile_hot, one_hot(named % 128, 128), NT, preferred_element_type=F32
        )
    for load in loads[1:]:
        load.wait()
    place_ref[...] = jnp.where(hits > 0.5, -1.0, row_ref[...].astype(F32))

    def terms(block, _):
        for inner in range(8):
            tile = block * 8 + inner
            lanes = pl.ds(pl.multiple_of(tile * 128, 128), 128)
            vel = vel_ref[:, lanes]
            volume = props_ref[0:1, lanes]
            force = props_ref[1:2, lanes] * (fluid_ref[:, lanes] - vel)
            moved = vel + drag_step * force / volume
            table_ref[pl.ds(tile * 8, 3), :] = force
            table_ref[pl.ds(tile * 8 + 3, 1), :] = volume
            table_ref[pl.ds(tile * 8 + 4, 3), :] = moved
            table_ref[pl.ds(tile * 8 + 7, 1), :] = height_ref[pl.ds(tile, 1), :].astype(F32)
        return 0

    lax.fori_loop(0, tiles // 8, terms, 0)
    tables = gather_table(table_ref, tiles, (0, 1, 2, 3, 7))
    for d in range(4):
        picked = gathered(tables, hot_ref[d], list_ref[d : d + 1, :])
        height_hot = one_hot(picked[4].astype(jnp.int32), 128)
        slot_ids = lax.broadcasted_iota(jnp.int32, (slots, movers), 0)
        at_slot = slot_ids == slot_ref[d : d + 1, :]
        spread = []
        for part in range(2):
            for f in range(4):
                value = two_parts(picked[f])[part].astype(F32)
                spread.append(jnp.where(at_slot, value, 0.0).astype(BF16))
        rows = lax.dot_general(
            jnp.concatenate(spread, axis=0), height_hot, NT, preferred_element_type=F32
        )
        packs[d][0 : 4 * slots, :] = rows[0 : 4 * slots] + rows[4 * slots : 8 * slots]
        at = 4 * slots
        packs[d][at : at + 8, :] = jnp.zeros((8, 128), F32)
        packs[d][at : at + 1, 0:slots] = ids_ref[d : d + 1, :].astype(F32)


def fibre_part(vel, fluid, props, row, height, lists, slots, ids):
    tiles = row.shape[0]
    movers = lists.shape[1]
    pack = (4 * ids.shape[1] + TILE, 128)
    ins = tuple(
        pltpu.with_memory_space_constraint(value, pltpu.HBM)
        for value in (vel, fluid, props, row, height, lists, slots, ids)
    )
    return call(
        fibre_kernel,
        [(tiles * 8, 128), (tiles, 128)] + [pack] * 4,
        ins,
        "fibre_terms",
        10**9,
        [HBM] * 8,
        [pltpu.VMEM(value.shape, value.dtype) for value in ins]
        + [pltpu.VMEM((4, 2 * tiles, movers), BF16), pltpu.SemaphoreType.DMA((8,))],
    )


def spread_tiles(table_ref, place_ref, values_ref, rows_ref, tiles):
    ids = lax.broadcasted_iota(jnp.int32, (16, 128), 0).astype(F32).astype(BF16)
    zero = jnp.zeros((16, 128), BF16)
    one = jnp.ones((16, 128), BF16)
    row_groups = rows_ref.shape[0] // 16
    for c in range(tiles):
        lanes = slice(c * 128, (c + 1) * 128)
        place = jnp.broadcast_to(place_ref[c : c + 1, :], (16, 128)).astype(BF16)
        for i in range(row_groups):
            rows_ref[16 * i : 16 * i + 16, lanes] = jnp.where(ids + BF16(16 * i) == place, one, zero)
        height = jnp.broadcast_to(table_ref[8 * c + 7 : 8 * c + 8, :], (16, 128)).astype(BF16)
        parts = []
        for f in range(4):
            parts.extend(two_parts(jnp.broadcast_to(table_ref[8 * c + f : 8 * c + f + 1, :], (16, 128))))
        for i in range(8):
            hit = ids + BF16(16 * i) == height
            for p in range(8):
                at = 128 * p + 16 * i
                values_ref[at : at + 16, lanes] = jnp.where(hit, parts[p], zero)


def deposit_kernel(table_ref, place_ref, out_ref, values_a, rows_a, values_b, rows_b, total, *, tiles, first, count):
    steps = count // tiles

    def fill(step, values, rows):
        spread_tiles(
            table_ref.at[pl.ds(pl.multiple_of((first + step * tiles) * 8, 8 * tiles), 8 * tiles), :],
            place_ref.at[pl.ds(pl.multiple_of(first + step * tiles, 8), tiles), :],
            values, rows, tiles,
        )

    def product(values, rows):
        return lax.dot_general(values[...], rows[...], NT, preferred_element_type=F32)

    fill(0, values_a, rows_a)
    part = product(values_a, rows_a)
    fill(1, values_b, rows_b)
    total[...] = part

    def pair(j, _):
        part = product(values_b, rows_b)
        fill(2 * j + 2, values_a, rows_a)
        total[...] += part
        part = product(values_a, rows_a)
        fill(2 * j + 3, values_b, rows_b)
        total[...] += part
        return 0

    lax.fori_loop(0, steps // 2 - 1, pair, 0)
    part = product(values_b, rows_b)
    for f in range(4):
        at = 256 * f
        out_ref[128 * f : 128 * f + 128, :] = (
            (total[at : at + 128, :] + part[at : at + 128, :])
            + (total[at + 128 : at + 256, :] + part[at + 128 : at + 256, :])
        )


def deposit_part(table, place, cells_x_y, first, count):
    tiles = DEPOSIT_TILES
    return pl.pallas_call(
        lambda *refs: deposit_kernel(*refs, tiles=tiles, first=first, count=count),
        out_shape=jax.ShapeDtypeStruct((512, cells_x_y), F32),
        scratch_shapes=[
            pltpu.VMEM((1024, 128 * tiles), BF16),
            pltpu.VMEM((cells_x_y, 128 * tiles), BF16),
            pltpu.VMEM((1024, 128 * tiles), BF16),
            pltpu.VMEM((cells_x_y, 128 * tiles), BF16),
            pltpu.VMEM((1024, cells_x_y), F32),
        ],
        compiler_params=pltpu.CompilerParams(vmem_limit_bytes=48 * MIB),
        cost_estimate=pl.CostEstimate(
            flops=17 * 10**9 * count // place.shape[0], bytes_accessed=MIB, transcendentals=0
        ),
        name="deposit",
    )(table, place)


def velocity_y_kernel(velocity_ref, heights_ref, mig_low, mig_high, beside_ref, low_ref, high_ref):
    x_width, y_width = velocity_ref.shape[1], velocity_ref.shape[2]
    base = mig_low.shape[0]
    low_ref[0:base, :] = mig_low[...]
    high_ref[0:base, :] = mig_high[...]
    beside = beside_rows(heights_ref[...])
    beside_ref[...] = beside
    fields = [flat(velocity_ref, f) for f in range(3)] + [beside]
    y_pack(fields, x_width, y_width, low_ref, high_ref, base)


def velocity_x_kernel(velocity_ref, beside_ref, above_ref, below_ref, mig_low, mig_high, low_ref, high_ref):
    x_width, y_width = velocity_ref.shape[1], velocity_ref.shape[2]
    base = mig_low.shape[0]
    low_ref[0:base, :] = mig_low[...]
    high_ref[0:base, :] = mig_high[...]
    fields = [flat(velocity_ref, f) for f in range(3)] + [beside_ref[...]]

    def halo(g, p):
        return y_halo(above_ref, below_ref, base, g, p, x_width)

    x_pack(fields, VELOCITY_DEPTHS, halo, x_width, y_width, low_ref, high_ref, base)


def arrived_rows(got, rows, slots):
    hots = []
    for d in range(4):
        named = got[d][4 * slots : 4 * slots + 1, 0:slots].astype(jnp.int32)
        hots.append(jnp.where(lax.broadcasted_iota(jnp.int32, (rows, slots), 0) == named, 1.0, 0.0))
    return jnp.concatenate(hots, axis=1)


def arrived_block(got, f, slots):
    return jnp.concatenate([got[d][f * slots : (f + 1) * slots, :] for d in range(4)], axis=0)


def face_kernel(*refs, slots, parts, first):
    parts_ref = refs[:parts]
    got = refs[parts : parts + 4]
    table_ref, place_ref, back_ref, out_ref, values_ref, rows_ref = refs[parts + 4 :]
    back = back_ref[0] > 0
    cells = rows_ref.shape[0]
    tiles = DEPOSIT_TILES
    ids = lax.broadcasted_iota(jnp.int32, (16, 128), 0).astype(F32).astype(BF16)
    zero = jnp.zeros((16, 128), BF16)
    one = jnp.ones((16, 128), BF16)
    lowest = jnp.where(back, 0.0, 112.0)

    def step(j, total):
        start = first + j * tiles
        table = table_ref.at[pl.ds(pl.multiple_of(start * 8, 8 * tiles), 8 * tiles), :]
        places = place_ref.at[pl.ds(pl.multiple_of(start, 8), tiles), :]
        for c in range(tiles):
            lanes = slice(c * 128, (c + 1) * 128)
            place = jnp.broadcast_to(places[c : c + 1, :], (16, 128)).astype(BF16)
            for i in range(cells // 16):
                rows_ref[16 * i : 16 * i + 16, lanes] = jnp.where(ids + BF16(16 * i) == place, one, zero)
            height = table[8 * c + 7 : 8 * c + 8, :] - lowest
            hit = ids == jnp.broadcast_to(height, (16, 128)).astype(BF16)
            for f in range(4):
                value = jnp.broadcast_to(table[8 * c + f : 8 * c + f + 1, :], (16, 128))
                for p, part in enumerate(two_parts(value)):
                    at = 64 * p + 16 * f
                    values_ref[at : at + 16, lanes] = jnp.where(hit, part, zero)
        return total + lax.dot_general(values_ref[...], rows_ref[...], NT, preferred_element_type=F32)

    count = (place_ref.shape[0] - first) // tiles
    total = lax.fori_loop(0, count, step, jnp.zeros((128, cells), F32))
    total = total[0:64] + total[64:128]
    blocks = []
    for f in range(4):
        turned = arrived_block(got, f, slots).T
        blocks.append(jnp.where(back, turned[0:TILE], turned[LANES - TILE : LANES]))
    arrived = lax.dot_general(
        jnp.concatenate(blocks, axis=0), arrived_rows(got, cells, slots), NT,
        preferred_element_type=F32, precision=lax.Precision.HIGHEST,
    )
    for f in range(4):
        low, high = 128 * f, 128 * f + LANES - TILE
        face = jnp.where(back, total[16 * f : 16 * f + 8], total[16 * f + 8 : 16 * f + 16])
        face = face + arrived[TILE * f : TILE * f + TILE]
        for ref in parts_ref:
            face = face + jnp.where(back, ref[low : low + TILE, :], ref[high : high + TILE, :])
        out_ref[TILE * f : TILE * f + TILE, :] = face


def total_kernel(*refs, slots, parts):
    parts_ref = refs[:parts]
    got = refs[parts : parts + 4]
    deposit_ref, = refs[parts + 4 :]
    hot = arrived_rows(got, deposit_ref.shape[1], slots)
    for f in range(4):
        at = 128 * f
        own = parts_ref[0][at : at + 128, :]
        for ref in parts_ref[1:]:
            own = own + ref[at : at + 128, :]
        deposit_ref[f] = own.T + jnp.dot(
            hot, arrived_block(got, f, slots), preferred_element_type=F32, precision=lax.Precision.HIGHEST
        )


def deposit_y_kernel(
    deposit_ref, heights_ref, mig_low, mig_high, beside_ref, low_ref, high_ref, *, x_width, y_width
):
    base = mig_low.shape[0]
    low_ref[0:base, :] = mig_low[...]
    high_ref[0:base, :] = mig_high[...]
    beside = beside_rows(heights_ref[...])
    beside_ref[...] = beside
    y_pack([deposit_ref[f] for f in range(4)] + [beside], x_width, y_width, low_ref, high_ref, base)


def deposit_x_kernel(
    deposit_ref, beside_ref, above_ref, below_ref, mig_low, mig_high, low_ref, high_ref, *, x_width, y_width
):
    base = mig_low.shape[0]
    low_ref[0:base, :] = mig_low[...]
    high_ref[0:base, :] = mig_high[...]

    def halo(g, p):
        return y_halo(above_ref, below_ref, base, g, p, x_width)

    fields = [deposit_ref[f] for f in range(4)] + [beside_ref[...]]
    x_pack(fields, DEPOSIT_DEPTHS, halo, x_width, y_width, low_ref, high_ref, base)


def partner_lanes(back, tall):
    lane = lax.broadcasted_iota(jnp.int32, (tall, LANES), 1)
    partner_at = jnp.where(back, LANES - SWEEPS, 0)
    return (lane >= partner_at) & (lane < partner_at + SWEEPS)


def beside_of(packed, f, back, partner):
    shift = jnp.where(back, LANES - TILE - TILE * f, (LANES - TILE * f) % LANES)
    return jnp.where(partner, pltpu.roll(packed, shift, axis=1), 0.0)


def outer_plane(ref, depths, start, g, k, tall):
    if k < 0 or k >= depths[g]:
        return jnp.zeros((tall, LANES), F32)
    at = start + tall * (sum(depths[:g]) + k)
    return ref[at : at + tall, :]


def plane_of(own, y_refs, x_refs, depths, start, g, plane, widths):
    x_width, y_width = widths
    tall = y_width + TILE
    x = plane - SWEEPS
    if x < 0:
        return outer_plane(x_refs[1], depths, start, g, x + depths[g], tall)
    if x >= x_width:
        return outer_plane(x_refs[0], depths, start, g, x - x_width, tall)
    return jnp.concatenate([own(g, x), y_halo(y_refs[0], y_refs[1], start, g, x, x_width)], axis=0)


def set_velocity(state, planes, get, back):
    partner = partner_lanes(back, state[0].shape[2])
    for p in planes:
        packed = get(3, p)
        for f in range(3):
            state[0][f, p] = jnp.concatenate([get(f, p), beside_of(packed, f, back, partner)], axis=1)


def set_source(state, planes, get, back):
    source, porosity = state[3], state[4]
    partner = partner_lanes(back, state[0].shape[2])
    for p in planes:
        packed = get(4, p)
        por = jnp.concatenate(
            [1.0 / (1.0 + get(3, p)), 1.0 / (1.0 + beside_of(packed, 3, back, partner))], axis=1
        )
        porosity[p] = por
        if 0 < p < porosity.shape[0] - 1:
            for f in range(3):
                drag = jnp.concatenate([get(f, p), beside_of(packed, f, back, partner)], axis=1)
                source[f, p] = por * state[0][f, p] - source_step * drag


def set_weights(state, first, last):
    porosity, w_x, w_y_low, w_y_high, w_z_low, w_z_high, scale = state[4:]
    tall = porosity.shape[1]

    def weights(p, _):
        por = porosity[p]
        low, high = 0.5 * (por + porosity[p - 1]), 0.5 * (por + porosity[p + 1])
        w_x[p - 1] = low
        w_x[p] = high
        total = low + high
        for ref, axis, shift in (
            (w_y_low, 0, 1), (w_y_high, 0, tall - 1), (w_z_low, 1, 1), (w_z_high, 1, 2 * LANES - 1),
        ):
            weight = 0.5 * (por + pltpu.roll(por, shift, axis=axis))
            ref[p] = weight
            total = total + weight
        scale[p] = 1.0 / (por + coupling * total)
        return 0

    lax.fori_loop(first, last, weights, 0)


def relax_planes(state, step, first, last, out_ref, back):
    source, _, w_x, w_y_low, w_y_high, w_z_low, w_z_high, scale = state[3:]
    old = state[step]
    tall = old.shape[2]
    inside = jnp.concatenate(
        [jnp.full((tall, LANES), 1.0, F32), jnp.where(partner_lanes(back, tall), 1.0, 0.0)], axis=1
    )

    def relax(p, _):
        for f in range(3):
            u = old[f, p]
            flux = w_x[p - 1] * old[f, p - 1] + w_x[p] * old[f, p + 1]
            flux = flux + w_y_low[p] * pltpu.roll(u, 1, axis=0)
            flux = flux + w_y_high[p] * pltpu.roll(u, tall - 1, axis=0)
            flux = flux + w_z_low[p] * pltpu.roll(u, 1, axis=1)
            flux = flux + w_z_high[p] * pltpu.roll(u, 2 * LANES - 1, axis=1)
            result = (source[f, p] + coupling * flux) * scale[p]
            if step < SWEEPS - 1:
                state[step + 1][f, p] = result * inside
            else:
                out_ref[f, p - SWEEPS] = result[0 : tall - TILE, 0:LANES]
        return 0

    lax.fori_loop(first, last, relax, 0)


def inner_kernel(
    velocity_ref, v_beside, v_above_y, v_below_y, v_above_x, v_below_x,
    deposit_ref, d_beside, d_above_y, d_below_y, back_ref, *state, v_base, d_base,
):
    widths = velocity_ref.shape[1], velocity_ref.shape[2]
    x_width, y_width = widths
    back = back_ref[0] > 0
    planes = x_width + 2 * SWEEPS

    def v_own(g, x):
        return velocity_ref[g, x] if g < 3 else v_beside[x * y_width : (x + 1) * y_width, :]

    def d_own(g, x):
        ref = deposit_ref.at[g] if g < 4 else d_beside
        return ref[x * y_width : (x + 1) * y_width, :]

    def velocity(g, p):
        return plane_of(
            v_own, (v_above_y, v_below_y), (v_above_x, v_below_x), VELOCITY_DEPTHS, v_base, g, p, widths
        )

    def deposit(g, p):
        return plane_of(d_own, (d_above_y, d_below_y), None, DEPOSIT_DEPTHS, d_base, g, p, widths)

    set_velocity(state, range(planes), velocity, back)
    set_source(state, range(SWEEPS, planes - SWEEPS), deposit, back)
    for step in range(SWEEPS - 1):
        first = SWEEPS + 1 + step
        if step == 0:
            set_weights(state, first, planes - first)
        relax_planes(state, step, first, planes - first, None, back)


def outer_kernel(
    above_y, below_y, above_x, below_x, back_ref, *refs, d_base, widths,
):
    state = refs[11 + 2 :]
    out_ref, arrivals_ref = refs[11], refs[12]
    x_width, y_width = widths
    back = back_ref[0] > 0
    planes = x_width + 2 * SWEEPS

    def deposit(g, p):
        return plane_of(None, None, (above_x, below_x), DEPOSIT_DEPTHS, d_base, g, p, widths)

    edge = tuple(range(SWEEPS)) + tuple(range(planes - SWEEPS, planes))
    set_source(state, edge, deposit, back)
    set_weights(state, 1, SWEEPS + 1)
    set_weights(state, planes - SWEEPS - 1, planes - 1)
    for step in range(SWEEPS - 1):
        relax_planes(state, step, step + 1, SWEEPS + 1 + step, None, back)
        relax_planes(state, step, planes - SWEEPS - 1 - step, planes - 1 - step, None, back)
    relax_planes(state, SWEEPS - 1, SWEEPS, planes - SWEEPS, out_ref, back)
    for d, got in enumerate((above_x, below_x, above_y, below_y)):
        at = 0
        for f in range(3):
            for t in range(arrivals_ref.shape[2] // 128):
                arrivals_ref[d, f : f + 1, t * 128 : (t + 1) * 128] = got[at : at + 1, :]
                at += 1


def moved_along(value, axis, steps):
    count = lax.axis_size(axis)
    return lax.ppermute(value, axis, [(i, (i + steps) % count) for i in range(count)])


def body(
    velocity, fibre_vel, fluid_vel, fibre_props, fibre_row, fibre_height, migrant_list, migrant_slot, side_rows,
):
    x_width, y_width = velocity.shape[1], velocity.shape[2]
    rows = x_width * y_width
    tall = y_width + TILE
    slots, movers = side_rows.shape[1], migrant_list.shape[1]
    back = lax.axis_index("gz").astype(jnp.int32).reshape(1)
    heights, = call(heights_kernel, [(3 * TILE, rows)], (velocity, back), "velocity_heights", 10**7, [VMEM, SMEM])
    v_heights = moved_along(heights, "gz", 1)
    table, place, *migs = fibre_part(
        fibre_vel, fluid_vel, fibre_props, fibre_row.reshape(-1, 128), fibre_height.reshape(-1, 128),
        migrant_list, migrant_slot, side_rows,
    )
    base = migs[0].shape[0]
    y_rows = base + 4 * rows // y_width * TILE // 2
    v_beside, low, high = call(
        velocity_y_kernel, [(rows, 128), (y_rows, 128), (y_rows, 128)], (velocity, v_heights, migs[2], migs[3]),
        "velocity_y_rows", 10**7,
    )
    counts = DEPOSIT_COUNTS
    firsts = [sum(counts[:k]) for k in range(len(counts))]
    v_above_y = moved_along(low, "gy", -1)
    v_below_y = moved_along(high, "gy", 1)
    part_0 = deposit_part(table, ordered(place, (low, high)), rows, firsts[0], counts[0])
    x_rows = base + tall * sum(VELOCITY_DEPTHS)
    low, high = call(
        velocity_x_kernel, [(x_rows, 128), (x_rows, 128)],
        (velocity, v_beside, v_above_y, ordered(v_below_y, part_0), migs[0], migs[1]), "velocity_x_planes", 10**7,
    )
    v_above_x = moved_along(low, "gx", -1)
    v_below_x = moved_along(high, "gx", 1)
    part_1 = deposit_part(table, ordered(place, (low, high)), rows, firsts[1], counts[1])
    arrived = (v_above_x, v_below_x, v_above_y, v_below_y)
    heights, = call(
        lambda *refs: face_kernel(*refs, slots=slots, parts=2, first=firsts[2]), [(4 * TILE, rows)],
        (part_0, part_1, *arrived, table, place, back), "deposit_face", 10**9, [VMEM] * 8 + [SMEM],
        [pltpu.VMEM((128, 128 * DEPOSIT_TILES), BF16), pltpu.VMEM((rows, 128 * DEPOSIT_TILES), BF16)],
    )
    d_heights = moved_along(heights, "gz", 1)
    part_2 = deposit_part(table, ordered(place, heights), rows, firsts[2], counts[2])
    deposit, = call(
        lambda *refs: total_kernel(*refs, slots=slots, parts=3), [(4, rows, 128)],
        (part_0, part_1, part_2, *arrived), "deposit_total", 10**7,
    )
    d_base = 3 * movers // 128
    mig_y = call(
        lambda *refs: movers_kernel(*refs, first=2), [(d_base, 128)] * 2,
        (ordered(table, part_2), migrant_list, place), "movers_y", 2 * 10**9,
    )
    y_rows = d_base + 5 * rows // y_width * TILE // 2
    d_beside, low, high = call(
        lambda *refs: deposit_y_kernel(*refs, x_width=x_width, y_width=y_width),
        [(rows, 128), (y_rows, 128), (y_rows, 128)], (deposit, d_heights, *mig_y), "deposit_y_rows", 10**7,
    )
    d_above_y = moved_along(low, "gy", -1)
    d_below_y = moved_along(high, "gy", 1)
    *mig_x, kept = call(
        lambda *refs: movers_kernel(*refs, first=0), [(d_base, 128)] * 2 + [fibre_vel.shape],
        (ordered(table, (low, high)), migrant_list, place), "movers_x", 2 * 10**9,
    )
    x_rows = d_base + tall * sum(DEPOSIT_DEPTHS)
    low, high = call(
        lambda *refs: deposit_x_kernel(*refs, x_width=x_width, y_width=y_width),
        [(x_rows, 128), (x_rows, 128)], (deposit, d_beside, d_above_y, d_below_y, *mig_x),
        "deposit_x_planes", 10**7,
    )
    d_above_x = moved_along(low, "gx", -1)
    d_below_x = moved_along(high, "gx", 1)
    planes = x_width + 2 * SWEEPS
    field, three = (planes, tall, 256), (3, planes, tall, 256)
    shapes = [three] * 4 + [field] * 7
    state = call(
        lambda *refs: inner_kernel(*refs, v_base=base, d_base=d_base), shapes,
        (
            velocity, v_beside, v_above_y, v_below_y, v_above_x, v_below_x,
            ordered(deposit, (low, high)), d_beside, d_above_y, d_below_y, back,
        ),
        "inner_sweeps", 2 * 10**9, [VMEM] * 10 + [SMEM], (), 24,
    )
    u, arrivals, *_ = pl.pallas_call(
        lambda *refs: outer_kernel(*refs, d_base=d_base, widths=(x_width, y_width)),
        out_shape=[jax.ShapeDtypeStruct(shape, F32) for shape in [velocity.shape, (4, 3, movers)] + shapes],
        in_specs=[VMEM] * 4 + [SMEM] + [VMEM] * 11,
        out_specs=[VMEM] * 13,
        input_output_aliases={5 + k: 2 + k for k in range(11)},
        compiler_params=pltpu.CompilerParams(vmem_limit_bytes=24 * MIB),
        cost_estimate=pl.CostEstimate(flops=10**8, bytes_accessed=2 * MIB, transcendentals=0),
        name="outer_sweeps",
    )(d_above_y, d_below_y, d_above_x, d_below_x, back, *state)
    return u, kept, arrivals


def solution(mesh):
    by_device = P(None, ("gx", "gy", "gz"))
    one_row = P(("gx", "gy", "gz"))
    grid = P(None, "gx", "gy", "gz")
    return jax.shard_map(
        body,
        mesh=mesh,
        in_specs=(grid, by_device, by_device, by_device, one_row, one_row, by_device, by_device, by_device),
        out_specs=(grid, by_device, P(None, None, ("gx", "gy", "gz"))),
        check_vma=False,
    )
```

```python
import jax
import jax.numpy as jnp
from jax import lax
from jax.experimental import pallas as pl
from jax.experimental.pallas import tpu as pltpu
from jax.sharding import PartitionSpec as P

F32 = jnp.float32
BF16 = jnp.bfloat16
NT = (((1,), (1,)), ((), ()))
drag_step = 0.25
source_step = 1.0
coupling = 1.0
SWEEPS = 3
TILE = 8
DEPOSIT_TILES = 8
DEPOSIT_COUNTS = (96, 128, 32)
LANES = 128
MIB = 2**20


def two_parts(value):
    high = value.astype(BF16)
    return high, (value - high.astype(F32)).astype(BF16)


def one_hot(index_row, count):
    ids = lax.broadcasted_iota(jnp.int32, (count, index_row.shape[1]), 0)
    return jnp.where(ids == index_row, 1.0, 0.0).astype(BF16)


def ordered(value, after):
    return lax.optimization_barrier((value, after))[0]


VMEM = pl.BlockSpec(memory_space=pltpu.VMEM)
SMEM = pl.BlockSpec(memory_space=pltpu.SMEM)
HBM = pl.BlockSpec(memory_space=pltpu.HBM)


def call(kernel, outs, ins, name, flops, in_specs=None, scratch=(), vmem=48):
    return pl.pallas_call(
        kernel,
        out_shape=[jax.ShapeDtypeStruct(shape, F32) for shape in outs],
        in_specs=in_specs or [VMEM] * len(ins),
        out_specs=[VMEM] * len(outs),
        scratch_shapes=list(scratch),
        compiler_params=pltpu.CompilerParams(vmem_limit_bytes=vmem * MIB),
        cost_estimate=pl.CostEstimate(flops=flops, bytes_accessed=2 * MIB, transcendentals=0),
        name=name,
    )(*ins)


def height_pack(fields, back_ref, out_ref):
    back = back_ref[0] > 0
    for f, field in enumerate(fields):
        turned = field.T
        out_ref[TILE * f : TILE * (f + 1), :] = jnp.where(
            back, turned[0:TILE, :], turned[LANES - TILE : LANES, :]
        )


def beside_rows(got):
    rest = jnp.zeros((LANES - got.shape[0], got.shape[1]), F32)
    return jnp.concatenate([got, rest], axis=0).T


def row_ids(width=LANES):
    return lax.broadcasted_iota(jnp.int32, (TILE, width), 0)


def y_pack(fields, x_width, y_width, low_ref, high_ref, base):
    half = x_width // 2
    ids = row_ids()
    for g, field in enumerate(fields):
        for p in range(half):
            at = base + (g * half + p) * TILE
            near, far = p * y_width, (p + half) * y_width
            low_ref[at : at + TILE, :] = jnp.where(
                ids < 4, field[near : near + TILE], pltpu.roll(field[far : far + TILE], 4, axis=0)
            )
            near, far = near + y_width - TILE, far + y_width - TILE
            high_ref[at : at + TILE, :] = jnp.where(
                ids < 4, pltpu.roll(field[far : far + TILE], 4, axis=0), field[near : near + TILE]
            )


def y_halo(above_ref, below_ref, base, g, p, x_width):
    half = x_width // 2
    at = base + (g * half + p % half) * TILE
    above, below = above_ref[at : at + TILE, :], below_ref[at : at + TILE, :]
    if p >= half:
        above, below = pltpu.roll(above, 4, axis=0), pltpu.roll(below, 4, axis=0)
    return jnp.where(row_ids() < 4, above, below)


def plane_rows(reach, g, k, from_low, y_width):
    depths, tails = reach
    distance = k + 1 if from_low else depths[g] - k
    return y_width + (TILE if distance <= tails[g] else 0)


def pack_rows(reach, y_width):
    return sum(plane_rows(reach, g, k, True, y_width) for g, depth in enumerate(reach[0]) for k in range(depth))


def x_pack(fields, reach, halo, x_width, y_width, low_ref, high_ref, base):
    for from_low, ref in ((True, low_ref), (False, high_ref)):
        at = base
        for g, field in enumerate(fields):
            depth = reach[0][g]
            for k in range(depth):
                plane = k if from_low else x_width - depth + k
                ref[at : at + y_width, :] = field[plane * y_width : (plane + 1) * y_width]
                rows = plane_rows(reach, g, k, from_low, y_width)
                if rows > y_width:
                    ref[at + y_width : at + rows, :] = halo(g, plane)
                at += rows


VELOCITY_REACH = ((3, 3, 3, 2), (2, 2, 2, 1))
DEPOSIT_REACH = ((2, 2, 2, 3, 2), (1, 1, 1, 2, 1))


def flat(ref, f):
    return ref[f].reshape(-1, LANES)


def heights_kernel(velocity_ref, back_ref, out_ref):
    height_pack([flat(velocity_ref, f) for f in range(3)], back_ref, out_ref)


def gather_table(table_ref, tiles, fields):
    stack = []
    for f in fields:
        high, low = two_parts(table_ref[pl.ds(f, tiles, stride=8), :].T)
        stack.append(jnp.concatenate([high, low], axis=1))
    return jnp.concatenate(stack, axis=0)


def gathered(tables, tile_hot, named):
    lane_hit = lax.broadcasted_iota(jnp.int32, (128, named.shape[1]), 0) == named % 128
    columns = jnp.dot(tables, tile_hot, preferred_element_type=F32)
    return [
        jnp.sum(jnp.where(lane_hit, columns[at : at + 128, :], 0.0), axis=0, keepdims=True)
        for at in range(0, columns.shape[0], 128)
    ]


def movers_kernel(table_ref, list_ref, place_ref, first_ref, second_ref, *kept, first):
    tiles = place_ref.shape[0]
    tables = gather_table(table_ref, tiles, (4, 5, 6))
    for d, out_ref in enumerate((first_ref, second_ref)):
        named = list_ref[first + d : first + d + 1, :]
        tile_hot = one_hot(named // 128, tiles)
        picked = gathered(tables, jnp.concatenate([tile_hot, tile_hot], axis=0), named)
        at = 0
        for f in range(3):
            for t in range(named.shape[1] // 128):
                out_ref[at : at + 1, :] = picked[f][:, t * 128 : (t + 1) * 128]
                at += 1
    if kept:

        def keep(block, _):
            for inner in range(8):
                tile = block * 8 + inner
                lanes = pl.ds(pl.multiple_of(tile * 128, 128), 128)
                stay = jnp.where(place_ref[pl.ds(tile, 1), :] < 0.0, 0.0, 1.0)
                kept[0][:, lanes] = table_ref[pl.ds(tile * 8 + 4, 3), :] * stay
            return 0

        lax.fori_loop(0, tiles // 8, keep, 0)


def fibre_kernel(
    vel_hbm, fluid_hbm, props_hbm, row_hbm, height_hbm, list_hbm, slot_hbm, ids_hbm,
    table_ref, place_ref, pack_0, pack_1, pack_2, pack_3,
    vel_ref, fluid_ref, props_ref, row_ref, height_ref, list_ref, slot_ref, ids_ref, hot_ref, arrived,
):
    loads = [
        pltpu.make_async_copy(source, target, arrived.at[k])
        for k, (source, target) in enumerate(
            (
                (list_hbm, list_ref), (row_hbm, row_ref), (vel_hbm, vel_ref), (fluid_hbm, fluid_ref),
                (props_hbm, props_ref), (height_hbm, height_ref), (slot_hbm, slot_ref),
                (ids_hbm, ids_ref),
            )
        )
    ]
    for load in loads:
        load.start()
    loads[0].wait()
    tiles = row_ref.shape[0]
    movers = list_ref.shape[1]
    packs = (pack_0, pack_1, pack_2, pack_3)
    slots = ids_ref.shape[1]
    hits = jnp.zeros((tiles, 128), F32)
    for d in range(4):
        named = list_ref[d : d + 1, :]
        tile_hot = one_hot(named // 128, tiles)
        hot_ref[d, 0:tiles, :] = tile_hot
        hot_ref[d, tiles : 2 * tiles, :] = tile_hot
        hits += lax.dot_general(
            tile_hot, one_hot(named % 128, 128), NT, preferred_element_type=F32
        )
    for load in loads[1:]:
        load.wait()
    place_ref[...] = jnp.where(hits > 0.5, -1.0, row_ref[...].astype(F32))

    def terms(block, _):
        for inner in range(8):
            tile = block * 8 + inner
            lanes = pl.ds(pl.multiple_of(tile * 128, 128), 128)
            vel = vel_ref[:, lanes]
            volume = props_ref[0:1, lanes]
            force = props_ref[1:2, lanes] * (fluid_ref[:, lanes] - vel)
            moved = vel + drag_step * force / volume
            table_ref[pl.ds(tile * 8, 3), :] = force
            table_ref[pl.ds(tile * 8 + 3, 1), :] = volume
            table_ref[pl.ds(tile * 8 + 4, 3), :] = moved
            table_ref[pl.ds(tile * 8 + 7, 1), :] = height_ref[pl.ds(tile, 1), :].astype(F32)
        return 0

    lax.fori_loop(0, tiles // 8, terms, 0)
    tables = gather_table(table_ref, tiles, (0, 1, 2, 3, 7))
    for d in range(4):
        picked = gathered(tables, hot_ref[d], list_ref[d : d + 1, :])
        height_hot = one_hot(picked[4].astype(jnp.int32), 128)
        slot_ids = lax.broadcasted_iota(jnp.int32, (slots, movers), 0)
        at_slot = slot_ids == slot_ref[d : d + 1, :]
        spread = []
        for part in range(2):
            for f in range(4):
                value = two_parts(picked[f])[part].astype(F32)
                spread.append(jnp.where(at_slot, value, 0.0).astype(BF16))
        rows = lax.dot_general(
            jnp.concatenate(spread, axis=0), height_hot, NT, preferred_element_type=F32
        )
        packs[d][0 : 4 * slots, :] = rows[0 : 4 * slots] + rows[4 * slots : 8 * slots]
        at = 4 * slots
        packs[d][at : at + 8, :] = jnp.zeros((8, 128), F32)
        packs[d][at : at + 1, 0:slots] = ids_ref[d : d + 1, :].astype(F32)


def fibre_part(vel, fluid, props, row, height, lists, slots, ids):
    tiles = row.shape[0]
    movers = lists.shape[1]
    pack = (4 * ids.shape[1] + TILE, 128)
    ins = tuple(
        pltpu.with_memory_space_constraint(value, pltpu.HBM)
        for value in (vel, fluid, props, row, height, lists, slots, ids)
    )
    return call(
        fibre_kernel,
        [(tiles * 8, 128), (tiles, 128)] + [pack] * 4,
        ins,
        "fibre_terms",
        10**9,
        [HBM] * 8,
        [pltpu.VMEM(value.shape, value.dtype) for value in ins]
        + [pltpu.VMEM((4, 2 * tiles, movers), BF16), pltpu.SemaphoreType.DMA((8,))],
    )


def spread_tiles(table_ref, place_ref, values_ref, rows_ref, tiles):
    ids = lax.broadcasted_iota(jnp.int32, (16, 128), 0).astype(F32).astype(BF16)
    zero = jnp.zeros((16, 128), BF16)
    one = jnp.ones((16, 128), BF16)
    row_groups = rows_ref.shape[0] // 16
    for c in range(tiles):
        lanes = slice(c * 128, (c + 1) * 128)
        place = jnp.broadcast_to(place_ref[c : c + 1, :], (16, 128)).astype(BF16)
        for i in range(row_groups):
            rows_ref[16 * i : 16 * i + 16, lanes] = jnp.where(ids + BF16(16 * i) == place, one, zero)
        height = jnp.broadcast_to(table_ref[8 * c + 7 : 8 * c + 8, :], (16, 128)).astype(BF16)
        parts = []
        for f in range(4):
            parts.extend(two_parts(jnp.broadcast_to(table_ref[8 * c + f : 8 * c + f + 1, :], (16, 128))))
        for i in range(8):
            hit = ids + BF16(16 * i) == height
            for p in range(8):
                at = 128 * p + 16 * i
                values_ref[at : at + 16, lanes] = jnp.where(hit, parts[p], zero)


def deposit_kernel(table_ref, place_ref, out_ref, values_a, rows_a, values_b, rows_b, total, *, tiles, first, count):
    steps = count // tiles

    def fill(step, values, rows):
        spread_tiles(
            table_ref.at[pl.ds(pl.multiple_of((first + step * tiles) * 8, 8 * tiles), 8 * tiles), :],
            place_ref.at[pl.ds(pl.multiple_of(first + step * tiles, 8), tiles), :],
            values, rows, tiles,
        )

    def product(values, rows):
        return lax.dot_general(values[...], rows[...], NT, preferred_element_type=F32)

    fill(0, values_a, rows_a)
    part = product(values_a, rows_a)
    fill(1, values_b, rows_b)
    total[...] = part

    def pair(j, _):
        part = product(values_b, rows_b)
        fill(2 * j + 2, values_a, rows_a)
        total[...] += part
        part = product(values_a, rows_a)
        fill(2 * j + 3, values_b, rows_b)
        total[...] += part
        return 0

    lax.fori_loop(0, steps // 2 - 1, pair, 0)
    part = product(values_b, rows_b)
    for f in range(4):
        at = 256 * f
        out_ref[128 * f : 128 * f + 128, :] = (
            (total[at : at + 128, :] + part[at : at + 128, :])
            + (total[at + 128 : at + 256, :] + part[at + 128 : at + 256, :])
        )


def deposit_part(table, place, cells_x_y, first, count):
    tiles = DEPOSIT_TILES
    return pl.pallas_call(
        lambda *refs: deposit_kernel(*refs, tiles=tiles, first=first, count=count),
        out_shape=jax.ShapeDtypeStruct((512, cells_x_y), F32),
        scratch_shapes=[
            pltpu.VMEM((1024, 128 * tiles), BF16),
            pltpu.VMEM((cells_x_y, 128 * tiles), BF16),
            pltpu.VMEM((1024, 128 * tiles), BF16),
            pltpu.VMEM((cells_x_y, 128 * tiles), BF16),
            pltpu.VMEM((1024, cells_x_y), F32),
        ],
        compiler_params=pltpu.CompilerParams(vmem_limit_bytes=48 * MIB),
        cost_estimate=pl.CostEstimate(
            flops=17 * 10**9 * count // place.shape[0], bytes_accessed=MIB, transcendentals=0
        ),
        name="deposit",
    )(table, place)


def velocity_y_kernel(velocity_ref, heights_ref, mig_low, mig_high, beside_ref, low_ref, high_ref):
    x_width, y_width = velocity_ref.shape[1], velocity_ref.shape[2]
    base = mig_low.shape[0]
    low_ref[0:base, :] = mig_low[...]
    high_ref[0:base, :] = mig_high[...]
    beside = beside_rows(heights_ref[...])
    beside_ref[...] = beside
    fields = [flat(velocity_ref, f) for f in range(3)] + [beside]
    y_pack(fields, x_width, y_width, low_ref, high_ref, base)


def velocity_x_kernel(velocity_ref, beside_ref, above_ref, below_ref, mig_low, mig_high, low_ref, high_ref):
    x_width, y_width = velocity_ref.shape[1], velocity_ref.shape[2]
    base = mig_low.shape[0]
    low_ref[0:base, :] = mig_low[...]
    high_ref[0:base, :] = mig_high[...]
    fields = [flat(velocity_ref, f) for f in range(3)] + [beside_ref[...]]

    def halo(g, p):
        return y_halo(above_ref, below_ref, base, g, p, x_width)

    x_pack(fields, VELOCITY_REACH, halo, x_width, y_width, low_ref, high_ref, base)


def arrived_rows(got, rows, slots):
    hots = []
    for d in range(4):
        named = got[d][4 * slots : 4 * slots + 1, 0:slots].astype(jnp.int32)
        hots.append(jnp.where(lax.broadcasted_iota(jnp.int32, (rows, slots), 0) == named, 1.0, 0.0))
    return jnp.concatenate(hots, axis=1)


def arrived_block(got, f, slots):
    return jnp.concatenate([got[d][f * slots : (f + 1) * slots, :] for d in range(4)], axis=0)


def face_kernel(*refs, slots, parts, first):
    parts_ref = refs[:parts]
    got = refs[parts : parts + 4]
    table_ref, place_ref, back_ref, out_ref, values_ref, rows_ref = refs[parts + 4 :]
    back = back_ref[0] > 0
    cells = rows_ref.shape[0]
    tiles = DEPOSIT_TILES
    ids = lax.broadcasted_iota(jnp.int32, (16, 128), 0).astype(F32).astype(BF16)
    zero = jnp.zeros((16, 128), BF16)
    one = jnp.ones((16, 128), BF16)
    lowest = jnp.where(back, 0.0, 112.0)

    def step(j, total):
        start = first + j * tiles
        table = table_ref.at[pl.ds(pl.multiple_of(start * 8, 8 * tiles), 8 * tiles), :]
        places = place_ref.at[pl.ds(pl.multiple_of(start, 8), tiles), :]
        for c in range(tiles):
            lanes = slice(c * 128, (c + 1) * 128)
            place = jnp.broadcast_to(places[c : c + 1, :], (16, 128)).astype(BF16)
            for i in range(cells // 16):
                rows_ref[16 * i : 16 * i + 16, lanes] = jnp.where(ids + BF16(16 * i) == place, one, zero)
            height = table[8 * c + 7 : 8 * c + 8, :] - lowest
            hit = ids == jnp.broadcast_to(height, (16, 128)).astype(BF16)
            for f in range(4):
                value = jnp.broadcast_to(table[8 * c + f : 8 * c + f + 1, :], (16, 128))
                for p, part in enumerate(two_parts(value)):
                    at = 64 * p + 16 * f
                    values_ref[at : at + 16, lanes] = jnp.where(hit, part, zero)
        return total + lax.dot_general(values_ref[...], rows_ref[...], NT, preferred_element_type=F32)

    count = (place_ref.shape[0] - first) // tiles
    total = lax.fori_loop(0, count, step, jnp.zeros((128, cells), F32))
    total = total[0:64] + total[64:128]
    blocks = []
    for f in range(4):
        turned = arrived_block(got, f, slots).T
        blocks.append(jnp.where(back, turned[0:TILE], turned[LANES - TILE : LANES]))
    arrived = lax.dot_general(
        jnp.concatenate(blocks, axis=0), arrived_rows(got, cells, slots), NT,
        preferred_element_type=F32, precision=lax.Precision.HIGHEST,
    )
    for f in range(4):
        low, high = 128 * f, 128 * f + LANES - TILE
        face = jnp.where(back, total[16 * f : 16 * f + 8], total[16 * f + 8 : 16 * f + 16])
        face = face + arrived[TILE * f : TILE * f + TILE]
        for ref in parts_ref:
            face = face + jnp.where(back, ref[low : low + TILE, :], ref[high : high + TILE, :])
        out_ref[TILE * f : TILE * f + TILE, :] = face


def total_kernel(*refs, slots, parts):
    parts_ref = refs[:parts]
    got = refs[parts : parts + 4]
    deposit_ref, = refs[parts + 4 :]
    hot = arrived_rows(got, deposit_ref.shape[1], slots)
    for f in range(4):
        at = 128 * f
        own = parts_ref[0][at : at + 128, :]
        for ref in parts_ref[1:]:
            own = own + ref[at : at + 128, :]
        deposit_ref[f] = own.T + jnp.dot(
            hot, arrived_block(got, f, slots), preferred_element_type=F32, precision=lax.Precision.HIGHEST
        )


def deposit_y_kernel(
    deposit_ref, heights_ref, mig_low, mig_high, beside_ref, low_ref, high_ref, *, x_width, y_width
):
    base = mig_low.shape[0]
    low_ref[0:base, :] = mig_low[...]
    high_ref[0:base, :] = mig_high[...]
    beside = beside_rows(heights_ref[...])
    beside_ref[...] = beside
    y_pack([deposit_ref[f] for f in range(4)] + [beside], x_width, y_width, low_ref, high_ref, base)


def deposit_x_kernel(
    deposit_ref, beside_ref, above_ref, below_ref, mig_low, mig_high, low_ref, high_ref, *, x_width, y_width
):
    base = mig_low.shape[0]
    low_ref[0:base, :] = mig_low[...]
    high_ref[0:base, :] = mig_high[...]

    def halo(g, p):
        return y_halo(above_ref, below_ref, base, g, p, x_width)

    fields = [deposit_ref[f] for f in range(4)] + [beside_ref[...]]
    x_pack(fields, DEPOSIT_REACH, halo, x_width, y_width, low_ref, high_ref, base)


def partner_lanes(back, tall):
    lane = lax.broadcasted_iota(jnp.int32, (tall, LANES), 1)
    partner_at = jnp.where(back, LANES - SWEEPS, 0)
    return (lane >= partner_at) & (lane < partner_at + SWEEPS)


def beside_of(packed, f, back, partner):
    shift = jnp.where(back, LANES - TILE - TILE * f, (LANES - TILE * f) % LANES)
    return jnp.where(partner, pltpu.roll(packed, shift, axis=1), 0.0)


def outer_plane(ref, reach, start, g, k, from_low, y_width):
    if k < 0 or k >= reach[0][g]:
        return jnp.zeros((y_width + TILE, LANES), F32)
    at = start
    for before in range(g + 1):
        for j in range(k if before == g else reach[0][before]):
            at += plane_rows(reach, before, j, from_low, y_width)
    rows = plane_rows(reach, g, k, from_low, y_width)
    plane = ref[at : at + rows, :]
    if rows > y_width:
        return plane
    return jnp.concatenate([plane, jnp.zeros((TILE, LANES), F32)], axis=0)


def plane_of(own, y_refs, x_refs, reach, start, g, plane, widths):
    x_width, y_width = widths
    x = plane - SWEEPS
    if x < 0:
        return outer_plane(x_refs[1], reach, start, g, x + reach[0][g], False, y_width)
    if x >= x_width:
        return outer_plane(x_refs[0], reach, start, g, x - x_width, True, y_width)
    return jnp.concatenate([own(g, x), y_halo(y_refs[0], y_refs[1], start, g, x, x_width)], axis=0)


def set_velocity(state, planes, get, back):
    partner = partner_lanes(back, state[0].shape[2])
    for p in planes:
        packed = get(3, p)
        for f in range(3):
            state[0][f, p] = jnp.concatenate([get(f, p), beside_of(packed, f, back, partner)], axis=1)


def set_source(state, planes, get, back):
    source, porosity = state[3], state[4]
    partner = partner_lanes(back, state[0].shape[2])
    for p in planes:
        packed = get(4, p)
        por = jnp.concatenate(
            [1.0 / (1.0 + get(3, p)), 1.0 / (1.0 + beside_of(packed, 3, back, partner))], axis=1
        )
        porosity[p] = por
        if 0 < p < porosity.shape[0] - 1:
            for f in range(3):
                drag = jnp.concatenate([get(f, p), beside_of(packed, f, back, partner)], axis=1)
                source[f, p] = por * state[0][f, p] - source_step * drag


def set_weights(state, first, last):
    porosity, w_x, w_y_low, w_y_high, w_z_low, w_z_high, scale = state[4:]
    tall = porosity.shape[1]

    def weights(p, _):
        por = porosity[p]
        low, high = 0.5 * (por + porosity[p - 1]), 0.5 * (por + porosity[p + 1])
        w_x[p - 1] = low
        w_x[p] = high
        total = low + high
        for ref, axis, shift in (
            (w_y_low, 0, 1), (w_y_high, 0, tall - 1), (w_z_low, 1, 1), (w_z_high, 1, 2 * LANES - 1),
        ):
            weight = 0.5 * (por + pltpu.roll(por, shift, axis=axis))
            ref[p] = weight
            total = total + weight
        scale[p] = 1.0 / (por + coupling * total)
        return 0

    lax.fori_loop(first, last, weights, 0)


def relax_planes(state, step, first, last, out_ref, back):
    source, _, w_x, w_y_low, w_y_high, w_z_low, w_z_high, scale = state[3:]
    old = state[step]
    tall = old.shape[2]
    inside = jnp.concatenate(
        [jnp.full((tall, LANES), 1.0, F32), jnp.where(partner_lanes(back, tall), 1.0, 0.0)], axis=1
    )

    def relax(p, _):
        for f in range(3):
            u = old[f, p]
            flux = w_x[p - 1] * old[f, p - 1] + w_x[p] * old[f, p + 1]
            flux = flux + w_y_low[p] * pltpu.roll(u, 1, axis=0)
            flux = flux + w_y_high[p] * pltpu.roll(u, tall - 1, axis=0)
            flux = flux + w_z_low[p] * pltpu.roll(u, 1, axis=1)
            flux = flux + w_z_high[p] * pltpu.roll(u, 2 * LANES - 1, axis=1)
            result = (source[f, p] + coupling * flux) * scale[p]
            if step < SWEEPS - 1:
                state[step + 1][f, p] = result * inside
            else:
                out_ref[f, p - SWEEPS] = result[0 : tall - TILE, 0:LANES]
        return 0

    lax.fori_loop(first, last, relax, 0)


def inner_kernel(
    velocity_ref, v_beside, v_above_y, v_below_y, v_above_x, v_below_x,
    deposit_ref, d_beside, d_above_y, d_below_y, back_ref, *state, v_base, d_base,
):
    widths = velocity_ref.shape[1], velocity_ref.shape[2]
    x_width, y_width = widths
    back = back_ref[0] > 0
    planes = x_width + 2 * SWEEPS

    def v_own(g, x):
        return velocity_ref[g, x] if g < 3 else v_beside[x * y_width : (x + 1) * y_width, :]

    def d_own(g, x):
        ref = deposit_ref.at[g] if g < 4 else d_beside
        return ref[x * y_width : (x + 1) * y_width, :]

    def velocity(g, p):
        return plane_of(
            v_own, (v_above_y, v_below_y), (v_above_x, v_below_x), VELOCITY_REACH, v_base, g, p, widths
        )

    def deposit(g, p):
        return plane_of(d_own, (d_above_y, d_below_y), None, DEPOSIT_REACH, d_base, g, p, widths)

    set_velocity(state, range(planes), velocity, back)
    set_source(state, range(SWEEPS, planes - SWEEPS), deposit, back)
    for step in range(SWEEPS - 1):
        first = SWEEPS + 1 + step
        if step == 0:
            set_weights(state, first, planes - first)
        relax_planes(state, step, first, planes - first, None, back)


def outer_kernel(
    above_y, below_y, above_x, below_x, back_ref, *refs, d_base, widths,
):
    state = refs[11 + 2 :]
    out_ref, arrivals_ref = refs[11], refs[12]
    x_width, y_width = widths
    back = back_ref[0] > 0
    planes = x_width + 2 * SWEEPS

    def deposit(g, p):
        return plane_of(None, None, (above_x, below_x), DEPOSIT_REACH, d_base, g, p, widths)

    edge = tuple(range(SWEEPS)) + tuple(range(planes - SWEEPS, planes))
    set_source(state, edge, deposit, back)
    set_weights(state, 1, SWEEPS + 1)
    set_weights(state, planes - SWEEPS - 1, planes - 1)
    for step in range(SWEEPS - 1):
        relax_planes(state, step, step + 1, SWEEPS + 1 + step, None, back)
        relax_planes(state, step, planes - SWEEPS - 1 - step, planes - 1 - step, None, back)
    relax_planes(state, SWEEPS - 1, SWEEPS, planes - SWEEPS, out_ref, back)
    for d, got in enumerate((above_x, below_x, above_y, below_y)):
        at = 0
        for f in range(3):
            for t in range(arrivals_ref.shape[2] // 128):
                arrivals_ref[d, f : f + 1, t * 128 : (t + 1) * 128] = got[at : at + 1, :]
                at += 1


def moved_along(value, axis, steps):
    count = lax.axis_size(axis)
    return lax.ppermute(value, axis, [(i, (i + steps) % count) for i in range(count)])


def body(
    velocity, fibre_vel, fluid_vel, fibre_props, fibre_row, fibre_height, migrant_list, migrant_slot, side_rows,
):
    x_width, y_width = velocity.shape[1], velocity.shape[2]
    rows = x_width * y_width
    tall = y_width + TILE
    slots, movers = side_rows.shape[1], migrant_list.shape[1]
    back = lax.axis_index("gz").astype(jnp.int32).reshape(1)
    heights, = call(heights_kernel, [(3 * TILE, rows)], (velocity, back), "velocity_heights", 10**7, [VMEM, SMEM])
    v_heights = moved_along(heights, "gz", 1)
    table, place, *migs = fibre_part(
        fibre_vel, fluid_vel, fibre_props, fibre_row.reshape(-1, 128), fibre_height.reshape(-1, 128),
        migrant_list, migrant_slot, side_rows,
    )
    base = migs[0].shape[0]
    y_rows = base + 4 * rows // y_width * TILE // 2
    v_beside, low, high = call(
        velocity_y_kernel, [(rows, 128), (y_rows, 128), (y_rows, 128)], (velocity, v_heights, migs[2], migs[3]),
        "velocity_y_rows", 10**7,
    )
    counts = DEPOSIT_COUNTS
    firsts = [sum(counts[:k]) for k in range(len(counts))]
    v_above_y = moved_along(low, "gy", -1)
    v_below_y = moved_along(high, "gy", 1)
    part_0 = deposit_part(table, ordered(place, (low, high)), rows, firsts[0], counts[0])
    x_rows = base + pack_rows(VELOCITY_REACH, y_width)
    low, high = call(
        velocity_x_kernel, [(x_rows, 128), (x_rows, 128)],
        (velocity, v_beside, v_above_y, ordered(v_below_y, part_0), migs[0], migs[1]), "velocity_x_planes", 10**7,
    )
    v_above_x = moved_along(low, "gx", -1)
    v_below_x = moved_along(high, "gx", 1)
    part_1 = deposit_part(table, ordered(place, (low, high)), rows, firsts[1], counts[1])
    arrived = (v_above_x, v_below_x, v_above_y, v_below_y)
    heights, = call(
        lambda *refs: face_kernel(*refs, slots=slots, parts=2, first=firsts[2]), [(4 * TILE, rows)],
        (part_0, part_1, *arrived, table, place, back), "deposit_face", 10**9, [VMEM] * 8 + [SMEM],
        [pltpu.VMEM((128, 128 * DEPOSIT_TILES), BF16), pltpu.VMEM((rows, 128 * DEPOSIT_TILES), BF16)],
    )
    d_heights = moved_along(heights, "gz", 1)
    part_2 = deposit_part(table, ordered(place, heights), rows, firsts[2], counts[2])
    deposit, = call(
        lambda *refs: total_kernel(*refs, slots=slots, parts=3), [(4, rows, 128)],
        (part_0, part_1, part_2, *arrived), "deposit_total", 10**7,
    )
    d_base = 3 * movers // 128
    mig_y = call(
        lambda *refs: movers_kernel(*refs, first=2), [(d_base, 128)] * 2,
        (ordered(table, part_2), migrant_list, place), "movers_y", 2 * 10**9,
    )
    y_rows = d_base + 5 * rows // y_width * TILE // 2
    d_beside, low, high = call(
        lambda *refs: deposit_y_kernel(*refs, x_width=x_width, y_width=y_width),
        [(rows, 128), (y_rows, 128), (y_rows, 128)], (deposit, d_heights, *mig_y), "deposit_y_rows", 10**7,
    )
    d_above_y = moved_along(low, "gy", -1)
    d_below_y = moved_along(high, "gy", 1)
    *mig_x, kept = call(
        lambda *refs: movers_kernel(*refs, first=0), [(d_base, 128)] * 2 + [fibre_vel.shape],
        (ordered(table, (low, high)), migrant_list, place), "movers_x", 2 * 10**9,
    )
    x_rows = d_base + pack_rows(DEPOSIT_REACH, y_width)
    low, high = call(
        lambda *refs: deposit_x_kernel(*refs, x_width=x_width, y_width=y_width),
        [(x_rows, 128), (x_rows, 128)], (deposit, d_beside, d_above_y, d_below_y, *mig_x),
        "deposit_x_planes", 10**7,
    )
    d_above_x = moved_along(low, "gx", -1)
    d_below_x = moved_along(high, "gx", 1)
    planes = x_width + 2 * SWEEPS
    field, three = (planes, tall, 256), (3, planes, tall, 256)
    shapes = [three] * 4 + [field] * 7
    state = call(
        lambda *refs: inner_kernel(*refs, v_base=base, d_base=d_base), shapes,
        (
            velocity, v_beside, v_above_y, v_below_y, v_above_x, v_below_x,
            ordered(deposit, (low, high)), d_beside, d_above_y, d_below_y, back,
        ),
        "inner_sweeps", 2 * 10**9, [VMEM] * 10 + [SMEM], (), 24,
    )
    u, arrivals, *_ = pl.pallas_call(
        lambda *refs: outer_kernel(*refs, d_base=d_base, widths=(x_width, y_width)),
        out_shape=[jax.ShapeDtypeStruct(shape, F32) for shape in [velocity.shape, (4, 3, movers)] + shapes],
        in_specs=[VMEM] * 4 + [SMEM] + [VMEM] * 11,
        out_specs=[VMEM] * 13,
        input_output_aliases={5 + k: 2 + k for k in range(11)},
        compiler_params=pltpu.CompilerParams(vmem_limit_bytes=24 * MIB),
        cost_estimate=pl.CostEstimate(flops=10**8, bytes_accessed=2 * MIB, transcendentals=0),
        name="outer_sweeps",
    )(d_above_y, d_below_y, d_above_x, d_below_x, back, *state)
    return u, kept, arrivals


def solution(mesh):
    by_device = P(None, ("gx", "gy", "gz"))
    one_row = P(("gx", "gy", "gz"))
    grid = P(None, "gx", "gy", "gz")
    return jax.shard_map(
        body,
        mesh=mesh,
        in_specs=(grid, by_device, by_device, by_device, one_row, one_row, by_device, by_device, by_device),
        out_specs=(grid, by_device, P(None, None, ("gx", "gy", "gz"))),
        check_vma=False,
    )
```
